256 devices in a mesh: section: 32 (over y, x, core), tensor: 8 (over z).
Axes of the slice: x: 4, y: 4, z: 8, core: 2. Of those that a mesh axis runs over, the one named last changes fastest.
Arguments:
- block_in: bfloat16 [4096, 4096], P('section', 'tensor'), may hold values from -6 to 6
- saved_in: bfloat16 [4096, 4096], P('section', 'tensor'), may hold values from -6 to 6
- block_grad: bfloat16 [4096, 4096], P('section', 'tensor'), may hold values from -6 to 6
- memory: bfloat16 [1024, 4096], P('section'), may hold values from -32 to 32
- norm_gain: float32 [32, 4096], P('section'), may hold values from 0.1 to 1.9
- w_query: bfloat16 [32, 4096, 2048], P('section', None, 'tensor'), may hold values from -1 to 1
- w_key: bfloat16 [32, 4096, 2048], P('section', None, 'tensor'), may hold values from -1 to 1
- w_value: bfloat16 [32, 4096, 2048], P('section', None, 'tensor'), may hold values from -0.75 to 0.75
- w_out: bfloat16 [32, 2048, 4096], P('section', 'tensor'), may hold values from -0.125 to 0.125
Outputs:
- next_block: bfloat16 [4096, 4096], P('section', 'tensor')
- prev_grad: bfloat16 [4096, 4096], P('section', 'tensor')
- memory_grad: float32 [1024, 4096], P('section', 'tensor')
The draws below stay inside these ranges and needn't reach their ends.
All inputs are finite; a program needn't handle non-finite values.
Results may differ from the reference program's by a relative error of at most 0.0085.
The reference program's roundings to bfloat16 on the way count: a program that leaves them out, or rounds other values in their place, can miss the bound.
Values may be sent and summed in bfloat16 or wider, within the bound.
No kernel may reach another device: no remote copies, remote signals or barrier semaphores. Data moves between devices by JAX's collectives and lax.ppermute only.
A program may use at most 128 MiB of HBM per device.

```python
import math
import jax
import jax.numpy as jnp
from jax import lax

D = 4096
HEAD_SIZE = 256
ROWS = 128
MEM = 1024
TGT = 4096
HW = 2048
N_SECTION = 32


def draw_block_in(key, part):
    own_key = jax.random.fold_in(key, 21)
    return jax.random.truncated_normal(own_key, -6.0, 6.0, (TGT, D), jnp.float32).astype(jnp.bfloat16)


def draw_saved_in(key, part):
    own_key = jax.random.fold_in(key, 22)
    return jax.random.truncated_normal(own_key, -6.0, 6.0, (TGT, D), jnp.float32).astype(jnp.bfloat16)


def draw_memory(key, part):
    own_key = jax.random.fold_in(key, 11)
    key_one = jax.random.fold_in(own_key, 0)
    return jax.random.truncated_normal(key_one, -6.0, 6.0, (MEM, D), jnp.float32).astype(jnp.bfloat16)


def draw_w_query(key, part):
    own_key = jax.random.fold_in(key, 31)
    values = jax.random.truncated_normal(own_key, -6.0, 6.0, (TGT // ROWS, D, HW), jnp.float32)
    return (values * D ** (-0.5)).astype(jnp.bfloat16)


def draw_w_key(key, part):
    own_key = jax.random.fold_in(key, 32)
    fresh = jax.random.truncated_normal(own_key, -6.0, 6.0, (TGT // ROWS, D, HW), jnp.float32)
    values = fresh
    return (values * D ** (-0.5)).astype(jnp.bfloat16)


def block_scale(stream_key, extent, cuts, least, top_value):
    level, own = 1.0, jax.random.fold_in(stream_key, 6)
    for position, shards_of in cuts:
        draws = jnp.exp(jax.random.uniform(jax.random.fold_in(own, position), (shards_of,), jnp.float32, least / len(cuts), top_value / len(cuts)))
        level = level * jnp.repeat(draws, extent[position] // shards_of).reshape([-1 if axis == position else 1 for axis in range(len(extent))])
    return level


def gaussian(key, shape, scale, limit, cuts=(), held_as=jnp.bfloat16):
    values = jax.random.normal(key, shape, jnp.float32) * scale
    if len(cuts) > 0:
        values = block_scale(key, shape, cuts, -0.22, 0.18) * values
    return jnp.clip(values, min=-limit, max=limit).astype(held_as)


def setup_inputs(seed: int = 0) -> dict:
    splits = jax.random.split(jax.random.key(seed), 10)
    return {
        "block_in": draw_block_in(jax.random.fold_in(splits[9], 71), 0),
        "saved_in": draw_saved_in(jax.random.fold_in(splits[9], 71), 0),
        "block_grad": gaussian(splits[2], (TGT, D), 1.0, 6.0, ((0, 32), (1, 8))),
        "memory": draw_memory(jax.random.fold_in(splits[9], 71), 0),
        "norm_gain": jnp.clip(1.0 + 0.18 * jax.random.normal(splits[4], (N_SECTION, D), jnp.float32), 0.1, 1.9),
        "w_query": draw_w_query(jax.random.fold_in(splits[9], 71), 0),
        "w_key": draw_w_key(jax.random.fold_in(splits[9], 71), 0),
        "w_value": gaussian(splits[7], (N_SECTION, D, HW), (8 * D ** -0.5), 0.75, ((0, 32), (2, 8))),
        "w_out": gaussian(splits[8], (N_SECTION, HW, D), HW ** -0.5, 0.125, ((0, 32), (1, 8))),
    }


def normalize(rows, gain):
    values = rows.astype(jnp.float32)
    factor = lax.rsqrt(lax.optimization_barrier(jnp.mean(values * values, axis=-1, keepdims=True)) + 1e-06)
    return ((values * factor * gain).astype(jnp.bfloat16), factor)

def attend_probs(query_matrix, projected_key_rows):
    headwise_queries = query_matrix.reshape(query_matrix.shape[0], -1, HEAD_SIZE).astype(jnp.float32)
    headwise_keys = projected_key_rows.reshape(projected_key_rows.shape[0], -1, HEAD_SIZE).astype(jnp.float32)
    score_matrix = jnp.einsum('ojn,ujn->jou', headwise_queries, headwise_keys) / math.sqrt(HEAD_SIZE)
    score_matrix = score_matrix - lax.optimization_barrier(jnp.max(score_matrix, axis=-1, keepdims=True))
    weights = jnp.exp(score_matrix)
    return weights / lax.optimization_barrier(jnp.sum(weights, axis=-1, keepdims=True))

def one_section(memory, inputs):
    input_rows, hidden_rows, g_rows, gain, wq, wk, wv, wo = inputs
    projected_key_rows = jnp.dot(memory, wk, preferred_element_type=jnp.float32).astype(jnp.bfloat16)
    projected_value_rows = jnp.dot(memory, wv, preferred_element_type=jnp.float32).astype(jnp.bfloat16)
    headwise_values = projected_value_rows.reshape(projected_value_rows.shape[0], -1, HEAD_SIZE).astype(jnp.float32)
    headwise_keys = projected_key_rows.reshape(projected_key_rows.shape[0], -1, HEAD_SIZE).astype(jnp.float32)
    normed, factor = normalize(input_rows, gain)
    query_matrix = jnp.dot(normed, wq, preferred_element_type=jnp.float32).astype(jnp.bfloat16)
    probability_batch = attend_probs(query_matrix, projected_key_rows).astype(jnp.bfloat16).astype(jnp.float32)
    attended_values = jnp.einsum('fox,xfi->ofi', probability_batch, headwise_values).reshape(input_rows.shape[0], -1).astype(jnp.bfloat16)
    layer_out = (input_rows.astype(jnp.float32) + jnp.dot(attended_values, wo, preferred_element_type=jnp.float32)).astype(jnp.bfloat16)
    normed_h, factor_h = normalize(hidden_rows, gain)
    query_per_head = jnp.dot(normed_h, wq, preferred_element_type=jnp.float32).astype(jnp.bfloat16)
    probs = attend_probs(query_per_head, projected_key_rows)
    probability_head_batch = probs.astype(jnp.bfloat16).astype(jnp.float32)
    attended_gradient = jnp.dot(g_rows, wo.T, preferred_element_type=jnp.float32).astype(jnp.bfloat16)
    headwise_attended_gradient = attended_gradient.reshape(attended_gradient.shape[0], -1, HEAD_SIZE).astype(jnp.float32)
    probability_gradient = jnp.einsum('ojn,ujn->jou', headwise_attended_gradient, headwise_values)
    d_score = probs * (probability_gradient - lax.optimization_barrier(jnp.sum(probs * probability_gradient, axis=-1, keepdims=True))) / math.sqrt(HEAD_SIZE)
    score_gradient_batch = d_score.astype(jnp.bfloat16).astype(jnp.float32)
    headwise_queries = query_per_head.reshape(query_per_head.shape[0], -1, HEAD_SIZE).astype(jnp.float32)
    query_gradient = jnp.einsum('fox,xfi->ofi', score_gradient_batch, headwise_keys).reshape(hidden_rows.shape[0], -1).astype(jnp.bfloat16)
    key_gradient = jnp.einsum('tuk,utz->ktz', score_gradient_batch, headwise_queries).reshape(memory.shape[0], -1).astype(jnp.bfloat16)
    value_gradient = jnp.einsum('tuk,utz->ktz', probability_head_batch, headwise_attended_gradient).reshape(memory.shape[0], -1).astype(jnp.bfloat16)
    d_normed = jnp.dot(query_gradient, wq.T, preferred_element_type=jnp.float32)
    h_vals = hidden_rows.astype(jnp.float32)
    inner = lax.optimization_barrier(jnp.mean(h_vals * gain * d_normed, axis=-1, keepdims=True))
    d_in = (g_rows.astype(jnp.float32) + factor_h * gain * d_normed - h_vals * factor_h ** 3 * inner).astype(jnp.bfloat16)
    d_memory = jnp.dot(key_gradient, wk.T, preferred_element_type=jnp.float32) + jnp.dot(value_gradient, wv.T, preferred_element_type=jnp.float32)
    return (layer_out, d_in, d_memory)

def reference(block_in, saved_in, block_grad, memory, norm_gain, w_query, w_key, w_value, w_out):
    sections = norm_gain.shape[0]
    width = block_in.shape[1]
    inputs = (block_in.reshape(sections, -1, width), saved_in.reshape(sections, -1, width), block_grad.reshape(sections, -1, width), norm_gain, w_query, w_key, w_value, w_out)

    def step(total, item):
        layer_out, d_in, d_memory = one_section(memory, item)
        return (total + d_memory, (layer_out, d_in))
    start = jnp.zeros(memory.shape, jnp.float32)
    memory_grad, (outs, grads) = lax.scan(step, start, inputs)
    blank = jnp.zeros((1,) + outs.shape[1:], jnp.bfloat16)
    next_block = jnp.concatenate([blank, outs[:-1]], axis=0).reshape(block_in.shape)
    prev_grad = jnp.concatenate([grads[1:], blank], axis=0).reshape(block_in.shape)
    return (next_block, prev_grad, memory_grad)
```

```python
import math

import jax
import jax.numpy as jnp
from jax import lax
from jax.sharding import PartitionSpec as P

HEAD_SIZE = 256
NY, NX, NC, NZ = 4, 4, 2, 8
AXES = ("section", "tensor")
BF = jnp.bfloat16
F32 = jnp.float32


def pairs_of(move):
    pairs = []
    for y in range(NY):
        for x in range(NX):
            for c in range(NC):
                for z in range(NZ):
                    ty, tx, tc, tz = move(y, x, c, z)
                    src = ((y * NX + x) * NC + c) * NZ + z
                    dst = (((ty % NY) * NX + tx % NX) * NC + tc % NC) * NZ + tz % NZ
                    pairs.append((src, dst))
    return pairs


def send(array, move):
    return lax.ppermute(array, AXES, pairs_of(move))


def first_axis(array, by):
    return send(array, lambda y, x, c, z: (y, x + by, c, z) if c == 0 else (y + by, x, c, z))


def second_axis(array, by):
    return send(array, lambda y, x, c, z: (y + by, x, c, z) if c == 0 else (y, x + by, c, z))


def other_core(array):
    return send(array, lambda y, x, c, z: (y, x, 1 - c, z))


def along_z(array, by):
    return send(array, lambda y, x, c, z: (y, x, c, z + by))


def shifted(x, by):
    devices = lax.axis_size("section")
    pairs = [(i, i + by) for i in range(devices) if 0 <= i + by < devices]
    return lax.ppermute(x, "section", pairs)


def row_factor(rows):
    values = rows.astype(F32)
    return lax.rsqrt(jnp.mean(values * values, axis=-1, keepdims=True) + 1e-06)


def matmul(left, right):
    return jnp.dot(left, right, preferred_element_type=F32)


def contract(left, right, dims):
    return lax.dot_general(left, right, ((dims[:1], dims[1:]), ((), ())), preferred_element_type=F32)


def softmax_probs(query, keys):
    scores = contract(query, keys, (1, 1)) / math.sqrt(HEAD_SIZE)
    scores = scores - jnp.max(scores, axis=-1, keepdims=True)
    weights = jnp.exp(scores)
    return weights / jnp.sum(weights, axis=-1, keepdims=True)


def ring_gather(block):
    down, up = block, block
    found = {0: block}
    half = block.shape[0] // 2
    for step in range(1, NZ // 2):
        up = along_z(up, -1)
        down = along_z(down, 1)
        found[step] = up
        found[NZ - step] = down
    first = along_z(up[:half], -1)
    second = along_z(down[half:], 1)
    found[NZ // 2] = jnp.concatenate([first, second], axis=0)
    return [found[i] for i in range(NZ)]


def body(block_in, saved_in, block_grad, memory, norm_gain, w_query, w_key, w_value, w_out):
    gain = norm_gain[0]
    wq, wk, wv, wo = w_query[0], w_key[0], w_value[0], w_out[0]
    rows, cols = block_in.shape
    width = wq.shape[0]
    place = lax.axis_index("tensor") * cols

    full_x = lax.all_gather(block_in, "tensor", axis=1, tiled=True)

    from_low, from_high = first_axis(memory, 1), first_axis(memory, -1)
    from_far = first_axis(memory, 2)
    near = jnp.concatenate([memory, from_low, from_high, from_far], axis=0)
    low, high = second_axis(near, 1), second_axis(near, -1)
    half = near.shape[0] // 2
    far = jnp.concatenate([second_axis(low[:half], 1), second_axis(high[half:], -1)], axis=0)
    wkv = jnp.concatenate([wk, wv], axis=1)
    pieces = [near, low, high, far]
    pieces = pieces + [other_core(piece) for piece in pieces]
    kv = jnp.concatenate([matmul(piece, wkv).astype(BF) for piece in pieces], axis=0)
    keys, values = kv[:, :HEAD_SIZE], kv[:, HEAD_SIZE:]

    both = jnp.concatenate(ring_gather(jnp.concatenate([saved_in, block_grad], axis=0)), axis=1)
    h_rel, g_rel = both[:rows], both[rows:]
    wq_rel = lax.dynamic_slice_in_dim(jnp.concatenate([wq, wq], axis=0), place, width, 0)
    wo_rel = lax.dynamic_slice_in_dim(jnp.concatenate([wo, wo], axis=1), place, width, 1)
    gain_rel = lax.dynamic_slice_in_dim(jnp.concatenate([gain, gain], axis=0), place, width, 0)
    wq_rel, wo_rel, gain_rel, wkv = lax.optimization_barrier((wq_rel, wo_rel, gain_rel, wkv))
    factor_h = row_factor(h_rel)
    normed_h = (h_rel.astype(F32) * factor_h * gain_rel).astype(BF)
    query_h_wide = matmul(normed_h, wq_rel)
    query_h = query_h_wide.astype(BF)
    d_att = contract(g_rel, wo_rel, (1, 1)).astype(BF)

    probs = softmax_probs(query_h, keys)
    d_probs = contract(d_att, values, (1, 1))
    d_score = probs * (d_probs - jnp.sum(probs * d_probs, axis=-1, keepdims=True)) / math.sqrt(HEAD_SIZE)
    d_score = d_score.astype(BF)
    d_query = matmul(d_score, keys).astype(BF)
    d_key = contract(d_score, query_h, (0, 0)).astype(BF)
    d_value = contract(probs.astype(BF), d_att, (0, 0)).astype(BF)
    d_kv = jnp.concatenate([d_key, d_value], axis=1)

    own = d_kv.shape[0] // 2
    piece_rows = own // 4
    arrived = other_core(contract(d_kv[own:], wkv, (1, 1)).astype(BF)).astype(F32)
    total = contract(d_kv[:own], wkv, (1, 1)) + arrived
    t_near, t_low, t_high, t_far = [total[i * piece_rows : (i + 1) * piece_rows] for i in range(4)]
    t_far = t_far.astype(BF)
    add_low = second_axis(t_far[:half], -1).astype(F32)
    add_high = second_axis(t_far[half:], 1).astype(F32)
    t_low = jnp.concatenate([t_low[:half] + add_low, t_low[half:]], axis=0).astype(BF)
    t_high = jnp.concatenate([t_high[:half], t_high[half:] + add_high], axis=0).astype(BF)
    t_near = t_near + second_axis(t_low, -1).astype(F32) + second_axis(t_high, 1).astype(F32)
    mine = memory.shape[0]
    wire = t_near[mine:].astype(BF)
    t_mine = (
        t_near[:mine]
        + first_axis(wire[:mine], -1).astype(F32)
        + first_axis(wire[mine : 2 * mine], 1).astype(F32)
        + first_axis(wire[2 * mine :], 2).astype(F32)
    )
    t_mine = lax.dynamic_slice_in_dim(jnp.concatenate([t_mine, t_mine], axis=1), place, width, 1)
    pair = t_mine[:, : 2 * cols]
    for by in (2, 4, 6):
        pair = pair + along_z(t_mine[:, by * cols : (by + 2) * cols].astype(BF), by).astype(F32)
    memory_grad = pair[:, :cols] + along_z(pair[:, cols:].astype(BF), 1).astype(F32)

    normed = (full_x.astype(F32) * row_factor(full_x) * gain).astype(BF)
    query = matmul(normed, wq).astype(BF)
    attended = matmul(softmax_probs(query, keys).astype(BF), values).astype(BF)
    branch = matmul(attended, wo)

    d_part = contract(d_query, wq, (1, 1))
    row_part = jnp.sum(d_query.astype(F32) * query_h_wide, axis=-1)
    row_part = jnp.zeros((16, cols), F32).at[0, :rows].set(row_part)
    split = lambda m: m.reshape(rows, NZ, cols).transpose(1, 0, 2)
    sent = jnp.concatenate(
        [split(d_part), split(branch), jnp.broadcast_to(row_part, (NZ, 16, cols))], axis=1
    ).astype(BF)
    summed = lax.psum_scatter(sent, "tensor", scatter_dimension=0, tiled=True)[0].astype(F32)
    d_cols, branch_cols = summed[:rows], summed[rows : 2 * rows]
    inner = summed[2 * rows, :rows][:, None] / factor_h / width
    layer_out = (block_in.astype(F32) + branch_cols).astype(BF)
    d_in = (
        block_grad.astype(F32)
        + factor_h * gain_rel[:cols] * d_cols
        - saved_in.astype(F32) * factor_h**3 * inner
    ).astype(BF)
    return shifted(layer_out, 1), shifted(d_in, -1), memory_grad


def solution(mesh):
    in_specs = (
        P("section", "tensor"),
        P("section", "tensor"),
        P("section", "tensor"),
        P("section", None),
        P("section", None),
        P("section", None, "tensor"),
        P("section", None, "tensor"),
        P("section", None, "tensor"),
        P("section", "tensor", None),
    )
    out_specs = (P("section", "tensor"), P("section", "tensor"), P("section", "tensor"))
    return jax.shard_map(body, mesh=mesh, in_specs=in_specs, out_specs=out_specs, check_vma=False)
```

```python
import functools
import math

import jax
import jax.numpy as jnp
from jax import lax
from jax.experimental import pallas as pl
from jax.experimental.pallas import tpu as pltpu
from jax.sharding import PartitionSpec as P

HEAD_SIZE = 256
NY, NX, NC, NZ = 4, 4, 2, 8
AXES = ("section", "tensor")
BF = jnp.bfloat16
F32 = jnp.float32


def pairs_of(move):
    pairs = []
    for y in range(NY):
        for x in range(NX):
            for c in range(NC):
                for z in range(NZ):
                    ty, tx, tc, tz = move(y, x, c, z)
                    src = ((y * NX + x) * NC + c) * NZ + z
                    dst = (((ty % NY) * NX + tx % NX) * NC + tc % NC) * NZ + tz % NZ
                    pairs.append((src, dst))
    return pairs


def send(array, move):
    return lax.ppermute(array, AXES, pairs_of(move))


def first_axis(array, by):
    return send(array, lambda y, x, c, z: (y, x + by, c, z) if c == 0 else (y + by, x, c, z))


def second_axis(array, by):
    return send(array, lambda y, x, c, z: (y + by, x, c, z) if c == 0 else (y, x + by, c, z))


def other_core(array):
    return send(array, lambda y, x, c, z: (y, x, 1 - c, z))


def along_z(array, by):
    return send(array, lambda y, x, c, z: (y, x, c, z + by))


def shifted(x, by):
    devices = lax.axis_size("section")
    pairs = [(i, i + by) for i in range(devices) if 0 <= i + by < devices]
    return lax.ppermute(x, "section", pairs)


def matmul(left, right):
    return jnp.dot(left, right, preferred_element_type=F32)


def contract(left, right, dims):
    return lax.dot_general(left, right, ((dims[:1], dims[1:]), ((), ())), preferred_element_type=F32)


def softmax_probs(query, keys):
    scores = contract(query, keys, (1, 1)) * (1.0 / math.sqrt(HEAD_SIZE))
    weights = jnp.exp(scores - jnp.max(scores, axis=-1, keepdims=True))
    return weights / jnp.sum(weights, axis=-1, keepdims=True)


def on_vmem(kernel, shapes, *operands, place=None, far_in=(), far_out=(), scratch=()):
    vmem, left = pl.BlockSpec(memory_space=pltpu.VMEM), pl.BlockSpec(memory_space=pl.ANY)
    first = [] if place is None else [pl.BlockSpec(memory_space=pltpu.SMEM)]
    outs = [jax.ShapeDtypeStruct(*shape) for shape in shapes]
    held = sum(max(a.size, 8 * 128) * a.dtype.itemsize for a in (*operands, *outs))
    call = pl.pallas_call(
        kernel,
        out_shape=outs,
        in_specs=first + [left if i in far_in else vmem for i in range(len(operands))],
        out_specs=[left if i in far_out else vmem for i in range(len(shapes))],
        scratch_shapes=list(scratch),
        compiler_params=pltpu.CompilerParams(vmem_limit_bytes=held + 3 * 2**20),
        cost_estimate=pl.CostEstimate(flops=2 * 10**9, bytes_accessed=held, transcendentals=0),
    )
    return call(*([] if place is None else [place]), *operands)


def stack_kernel(*refs):
    (*parts, out_ref), held, sems = refs[:-2], refs[-2], refs[-1]
    copies, start = [], 0
    for i, ref in enumerate(parts):
        at = pl.ds(start, ref.shape[0])
        into = pltpu.make_async_copy(ref, held.at[at], sems.at[i])
        copies.append((into, pltpu.make_async_copy(held.at[at], out_ref.at[at], sems.at[len(parts) + i])))
        start += ref.shape[0]
    for into, _ in copies:
        into.start()
    for into, out in copies:
        into.wait()
        out.start()
    for _, out in copies:
        out.wait()


def stack(*parts):
    shape = (sum(part.shape[0] for part in parts), parts[0].shape[1])
    hbm = pl.BlockSpec(memory_space=pl.ANY)
    return pl.pallas_call(
        stack_kernel,
        out_shape=jax.ShapeDtypeStruct(shape, parts[0].dtype),
        in_specs=[hbm] * len(parts),
        out_specs=hbm,
        scratch_shapes=[pltpu.VMEM(shape, parts[0].dtype), pltpu.SemaphoreType.DMA((2 * len(parts),))],
        cost_estimate=pl.CostEstimate(flops=1, bytes_accessed=1, transcendentals=0),
    )(*parts)


def project_kernel(
    far_ref, gain_ref, wq_ref, wo_ref, query_x_ref, query_ref, wide_ref, d_att_ref, factor_ref, all_ref, sems
):
    rows = wide_ref.shape[0]
    cols = all_ref.shape[1] // NZ
    copies = []
    for k in range(NZ):
        at = pl.ds(k * cols, cols)
        copies.append(pltpu.make_async_copy(far_ref.at[:, at], all_ref.at[:, at], sems.at[k]))
        copies[k].start()
    squares = [jnp.zeros((rows, cols), F32) for _ in range(2)]
    d_att = jnp.zeros(wide_ref.shape, F32)
    for k in range(NZ):
        at = slice(k * cols, (k + 1) * cols)
        copies[k].wait()
        for block in range(2):
            wide = all_ref[block * rows : (block + 1) * rows, at].astype(F32)
            squares[block] = squares[block] + wide * wide
        d_att = d_att + contract(all_ref[2 * rows :, at], wo_ref[:, at], (1, 1))
    d_att_ref[...] = d_att.astype(BF)
    factors = []
    for block in range(2):
        mean = jnp.sum(squares[block], axis=-1, keepdims=True) * (1.0 / (NZ * cols))
        factors.append(lax.rsqrt(mean + 1e-06))
    factor_ref[...] = factors[1]
    query_x = jnp.zeros(wide_ref.shape, F32)
    query_h = jnp.zeros(wide_ref.shape, F32)
    for k in range(NZ):
        at = slice(k * cols, (k + 1) * cols)
        gain = gain_ref[:, at]
        normed_x = (all_ref[:rows, at].astype(F32) * factors[0] * gain).astype(BF)
        normed_h = (all_ref[rows : 2 * rows, at].astype(F32) * factors[1] * gain).astype(BF)
        query_x = query_x + matmul(normed_x, wq_ref[at, :])
        query_h = query_h + matmul(normed_h, wq_ref[at, :])
    query_x_ref[...] = query_x.astype(BF)
    query_ref[...] = query_h.astype(BF)
    wide_ref[...] = query_h


def backward_kernel(kv_ref, query_ref, wide_ref, d_att_ref, d_key_ref, d_value_ref, d_query_ref, extra_ref):
    keys = kv_ref[:, :HEAD_SIZE]
    query, d_att = query_ref[...], d_att_ref[...]
    probs = softmax_probs(query, keys)
    d_probs = contract(d_att, kv_ref[:, HEAD_SIZE:], (1, 1))
    inner = jnp.sum(probs * d_probs, axis=-1, keepdims=True)
    d_score = (probs * (d_probs - inner) * (1.0 / math.sqrt(HEAD_SIZE))).astype(BF)
    d_key_ref[...] = contract(d_score, query, (0, 0)).astype(BF)
    d_value_ref[...] = contract(probs.astype(BF), d_att, (0, 0)).astype(BF)
    d_query = matmul(d_score, keys).astype(BF)
    d_query_ref[...] = d_query
    product = d_query.astype(F32) * wide_ref[...]
    sums = lax.dot_general(
        jnp.ones((extra_ref.shape[0], product.shape[1]), F32),
        product,
        (((1,), (1,)), ((), ())),
        precision=lax.Precision.HIGHEST,
        preferred_element_type=F32,
    )
    extra_ref[...] = jnp.zeros(extra_ref.shape, BF)
    extra_ref[:, : sums.shape[1]] = sums.astype(BF)


def memory_part(d_key, d_value, wk_ref, wv_ref, out_refs, *added):
    width, tile = wk_ref.shape[0], 512

    def tile_of(refs, k):
        ref = refs[k * tile * len(refs) // width]
        at = k * tile % ref.shape[1]
        return ref, slice(at, at + tile)

    for k in range(width // tile):
        at = slice(k * tile, (k + 1) * tile)
        part = contract(d_key, wk_ref[at, :], (1, 1)) + contract(d_value, wv_ref[at, :], (1, 1))
        for refs in added:
            ref, cols = tile_of(refs, k)
            part = part + ref[:, cols].astype(F32)
        ref, cols = tile_of(out_refs, k)
        ref[:, cols] = part.astype(ref.dtype)


def heads_kernel(query_ref, wq_ref, wo_ref, kv_ref, d_query_ref, extra_ref, far_ref, out_ref, sems):
    rows, cols = query_ref.shape[0], out_ref.shape[2]
    probs = softmax_probs(query_ref[...], kv_ref[:, :HEAD_SIZE]).astype(BF)
    attended = matmul(probs, kv_ref[:, HEAD_SIZE:]).astype(BF)
    d_query = d_query_ref[...]
    copies = []
    for k in range(NZ):
        at = slice(k * cols, (k + 1) * cols)
        out_ref[k, :rows] = contract(d_query, wq_ref[at, :], (1, 1)).astype(BF)
        out_ref[k, rows : 2 * rows] = matmul(attended, wo_ref[:, at]).astype(BF)
        out_ref[k, 2 * rows :] = extra_ref[...]
        copies.append(pltpu.make_async_copy(out_ref.at[k], far_ref.at[k], sems.at[k]))
        copies[k].start()
    for copy in copies:
        copy.wait()


def finish_kernel(place_ref, sums_ref, x_ref, h_ref, g_ref, factor_ref, gain_ref, layer_ref, d_in_ref):
    rows, cols = x_ref.shape
    layer_ref[...] = (x_ref[...].astype(F32) + sums_ref[rows : 2 * rows].astype(F32)).astype(BF)
    factor = factor_ref[...]
    at = pl.multiple_of(place_ref[0] * cols, cols)
    gain = gain_ref[:, pl.ds(at, cols)]
    eye = lax.broadcasted_iota(jnp.int32, (rows, rows), 0) == lax.broadcasted_iota(jnp.int32, (rows, rows), 1)
    inner = contract(jnp.where(eye, 1.0, 0.0).astype(BF), sums_ref[2 * rows :, :rows], (1, 1))[:, :1]
    inner = inner / factor * (1.0 / (NZ * cols))
    d_in = g_ref[...].astype(F32) + factor * gain * sums_ref[:rows].astype(F32)
    d_in_ref[...] = (d_in - h_ref[...].astype(F32) * (factor * factor * factor * inner)).astype(BF)


def cross_kernel(blocks, d_key_ref, d_value_ref, wk_ref, wv_ref, *out_refs):
    for i, ref in zip(blocks, out_refs):
        at = slice((4 + i) * ref.shape[0], (5 + i) * ref.shape[0])
        memory_part(d_key_ref[at], d_value_ref[at], wk_ref, wv_ref, [ref])


def halves_kernel(columns_from, d_key_ref, d_value_ref, wk_ref, wv_ref, *refs):
    rows = refs[-1].shape[0]
    at = slice(columns_from * rows, (columns_from + 1) * rows)
    memory_part(d_key_ref[at], d_value_ref[at], wk_ref, wv_ref, refs[-2:], refs[:-2])


def middle_kernel(d_key_ref, d_value_ref, wk_ref, wv_ref, low_ref, high_ref, out_low, out_high):
    rows, cols = out_low.shape
    width, tile = wk_ref.shape[0], 512
    for block, ref, arrived, start in ((1, out_low, low_ref, cols), (2, out_high, high_ref, 0)):
        rows_at = slice(block * rows, (block + 1) * rows)
        for k in range(cols // tile):
            at = slice(start + k * tile, start + (k + 1) * tile)
            part = contract(d_key_ref[rows_at], wk_ref[at, :], (1, 1))
            part = part + contract(d_value_ref[rows_at], wv_ref[at, :], (1, 1))
            ref[:, k * tile : (k + 1) * tile] = (part + arrived[:, at].astype(F32)).astype(ref.dtype)


def edge_kernel(d_key_ref, d_value_ref, wk_ref, wv_ref, low_ref, high_ref, add_low, add_high, out_low, out_high):
    rows, cols = out_low.shape
    width, tile = wk_ref.shape[0], 512
    for block, ref, arrived, add, start in ((1, out_low, low_ref, add_low, 0), (2, out_high, high_ref, add_high, cols)):
        rows_at = slice(block * rows, (block + 1) * rows)
        for k in range(cols // tile):
            at = slice(start + k * tile, start + (k + 1) * tile)
            here = slice(k * tile, (k + 1) * tile)
            part = contract(d_key_ref[rows_at], wk_ref[at, :], (1, 1))
            part = part + contract(d_value_ref[rows_at], wv_ref[at, :], (1, 1))
            part = part + arrived[:, at].astype(F32) + add[:, here].astype(F32)
            ref[:, here] = part.astype(ref.dtype)


def near_kernel(
    d_key_ref, d_value_ref, wk_ref, wv_ref, arrived_ref, low_a, low_b, high_a, high_b, mine_ref, *wires
):
    mine, rows = mine_ref.shape[0], arrived_ref.shape[0]
    width, tile = wk_ref.shape[0], 512
    cols = low_a.shape[1]
    for k in range(width // tile):
        at = slice(k * tile, (k + 1) * tile)
        part = contract(d_key_ref[:rows], wk_ref[at, :], (1, 1)) + contract(d_value_ref[:rows], wv_ref[at, :], (1, 1))
        low, high = (low_a, high_a) if k * tile < cols else (low_b, high_b)
        here = slice(k * tile % cols, k * tile % cols + tile)
        part = part + arrived_ref[:, at].astype(F32) + low[:, here].astype(F32) + high[:, here].astype(F32)
        for i, ref in enumerate((mine_ref, *wires)):
            ref[:, at] = part[i * mine : (i + 1) * mine].astype(ref.dtype)


def assemble_kernel(a_ref, b_ref, c_ref, d_ref, first_ref, second_ref, near_ref):
    mine, cols = a_ref.shape[0], first_ref.shape[1]
    for i, ref in enumerate((a_ref, b_ref, c_ref, d_ref)):
        at = slice(i * mine, (i + 1) * mine)
        first_ref[at] = ref[:, :cols]
        second_ref[at] = ref[:, cols:]
        near_ref[at] = ref[...]


def keys_kernel(*refs):
    *pieces, wk_ref, wv_ref, out_ref = refs
    rows, width, tile = pieces[0].shape[0], wk_ref.shape[0], 1024
    blocks = []
    while pieces:
        count = width // pieces[0].shape[1]
        blocks.append(pieces[:count])
        pieces = pieces[count:]
    for i, block in enumerate(blocks):
        for w_ref, at in ((wk_ref, 0), (wv_ref, HEAD_SIZE)):
            total = jnp.zeros((rows, HEAD_SIZE), F32)
            for k in range(width // tile):
                ref = block[k * tile * len(block) // width]
                here = k * tile % ref.shape[1]
                total = total + matmul(ref[:, here : here + tile], w_ref[k * tile : (k + 1) * tile, :])
            out_ref[i * rows : (i + 1) * rows, at : at + HEAD_SIZE] = total.astype(BF)


def spread_kernel(place_ref, mine_ref, a_ref, b_ref, c_ref, pair_ref, *rest):
    outs, total_ref = rest[:-1], rest[-1]
    total_ref[...] = (
        mine_ref[...] + a_ref[...].astype(F32) + b_ref[...].astype(F32) + c_ref[...].astype(F32)
    )
    cols = total_ref.shape[1] // NZ
    for i, ref in enumerate((pair_ref, *outs)):
        for j in range(2):
            at = pl.multiple_of(lax.rem(place_ref[0] + 2 * i + j, NZ) * cols, cols)
            ref[:, j * cols : (j + 1) * cols] = total_ref[:, pl.ds(at, cols)].astype(ref.dtype)


def pair_kernel(pair_ref, a_ref, b_ref, c_ref, block_ref, grad_ref, own_ref, next_ref):
    total = pair_ref[...] + a_ref[...].astype(F32) + b_ref[...].astype(F32) + c_ref[...].astype(F32)
    cols = own_ref.shape[1]
    own_ref[...] = total[:, :cols]
    next_ref[...] = total[:, cols:].astype(BF)


def body(block_in, saved_in, block_grad, memory, norm_gain, w_query, w_key, w_value, w_out):
    rows, cols = block_in.shape
    width, size = w_query.shape[1:]
    at_z = lax.axis_index("tensor").reshape(1)

    gathered = lax.all_gather(stack(block_in, saved_in, block_grad), "tensor", axis=1, tiled=True)
    wq, wk, wv, wo = w_query[0], w_key[0], w_value[0], w_out[0]

    mem = NY * NX * NC * memory.shape[0]
    quarter = mem // 8
    half = ((quarter, width // 2), BF)
    near_a, near_b, near = on_vmem(
        assemble_kernel, [half] * 2 + [((quarter, width), BF)], memory, first_axis(memory, 1), first_axis(memory, -1), first_axis(memory, 2)
    )
    low_a, high_b = second_axis(near_a, 1), second_axis(near_b, -1)
    low_b, high_a = second_axis(near_b, 1), second_axis(near_a, -1)
    far_a, far_b = second_axis(low_a, 1), second_axis(high_b, -1)

    near_sent, low_a, high_b = lax.optimization_barrier((near, low_a, high_b))
    others = [other_core(piece) for piece in (near_sent, low_a, low_b, high_a, high_b)]

    def keys_of(*pieces):
        blocks = sum(piece.shape[1] for piece in pieces) // width
        return on_vmem(keys_kernel, [((blocks * quarter, 2 * size), BF)], *pieces, wk, wv)[0]

    kv = jnp.concatenate([
        keys_of(near, low_a, low_b, high_a, high_b),
        keys_of(far_a, far_b),
        keys_of(*others),
        keys_of(other_core(far_a), other_core(far_b)),
    ], axis=0)

    query_x, query_h, wide_h, d_att, factor_h = on_vmem(
        project_kernel,
        [((rows, size), BF), ((rows, size), BF), ((rows, size), F32), ((rows, size), BF), ((rows, 1), F32)],
        gathered, norm_gain, wq, wo,
        far_in=(0,),
        scratch=[pltpu.VMEM(gathered.shape, BF), pltpu.SemaphoreType.DMA((NZ,))],
    )
    d_key, d_value, d_query, extra = on_vmem(
        backward_kernel,
        [((mem, size), BF), ((mem, size), BF), ((rows, size), BF), ((16, cols), BF)],
        kv, query_h, wide_h, d_att,
    )
    own = (d_key, d_value, wk, wv)
    whole = ((quarter, width), BF)
    far, low = on_vmem(functools.partial(cross_kernel, (3, 1)), [whole] * 2, *own)
    high, near = on_vmem(functools.partial(cross_kernel, (2, 0)), [whole] * 2, *own)
    shape = (NZ, 2 * rows + 16, cols)
    (sent,) = on_vmem(
        heads_kernel, [(shape, BF)], query_x, wq, wo, kv, d_query, extra,
        far_out=(0,),
        scratch=[pltpu.VMEM(shape, BF), pltpu.SemaphoreType.DMA((NZ,))],
    )
    summed = lax.psum_scatter(sent, "tensor", scatter_dimension=0, tiled=True)[0]
    layer_out, d_in = on_vmem(
        finish_kernel, [((rows, cols), BF)] * 2, summed, block_in, saved_in, block_grad, factor_h, norm_gain,
        place=at_z,
    )
    next_block, prev_grad = shifted(layer_out, 1), shifted(d_in, -1)

    far, low, high, near = other_core(far), other_core(low), other_core(high), other_core(near)
    mine = memory.shape[0]
    far_a, far_b = on_vmem(functools.partial(halves_kernel, 3), [half] * 2, *own, far)
    low_b, high_a = on_vmem(middle_kernel, [half] * 2, *own, low, high)
    back_low_b, back_high_a = second_axis(low_b, -1), second_axis(high_a, 1)
    low_a, high_b = on_vmem(
        edge_kernel, [half] * 2, *own, low, high, second_axis(far_a, -1), second_axis(far_b, 1)
    )
    back_low_a, back_high_b = second_axis(low_a, -1), second_axis(high_b, 1)
    t_mine, *wires = on_vmem(
        near_kernel,
        [((mine, width), F32)] + [((mine, width), BF)] * 3,
        *own, near, back_low_a, back_low_b, back_high_a, back_high_b,
    )
    arrived = [first_axis(wires[0], -1), first_axis(wires[1], 1), first_axis(wires[2], 2)]
    pair, *wires = on_vmem(
        spread_kernel,
        [((mine, 2 * cols), F32)] + [((mine, 2 * cols), BF)] * 3,
        t_mine, *arrived,
        place=at_z,
        scratch=[pltpu.VMEM((mine, width), F32)],
    )
    arrived = [along_z(wire, by) for wire, by in zip(wires, (2, 4, 6))]
    own_cols, next_cols = on_vmem(
        pair_kernel, [((mine, cols), F32), ((mine, cols), BF)], pair, *arrived, next_block, prev_grad
    )
    memory_grad = own_cols + along_z(next_cols, 1).astype(F32)

    return next_block, prev_grad, memory_grad


def solution(mesh):
    in_specs = (
        P("section", "tensor"),
        P("section", "tensor"),
        P("section", "tensor"),
        P("section", None),
        P("section", None),
        P("section", None, "tensor"),
        P("section", None, "tensor"),
        P("section", None, "tensor"),
        P("section", "tensor", None),
    )
    out_specs = (P("section", "tensor"), P("section", "tensor"), P("section", "tensor"))
    return jax.shard_map(body, mesh=mesh, in_specs=in_specs, out_specs=out_specs, check_vma=False)
```

```python
import functools
import math

import jax
import jax.numpy as jnp
from jax import lax
from jax.experimental import pallas as pl
from jax.experimental.pallas import tpu as pltpu
from jax.sharding import PartitionSpec as P

HEAD_SIZE = 256
NY, NX, NC, NZ = 4, 4, 2, 8
AXES = ("section", "tensor")
BF = jnp.bfloat16
F32 = jnp.float32


def pairs_of(move):
    pairs = []
    for y in range(NY):
        for x in range(NX):
            for c in range(NC):
                for z in range(NZ):
                    ty, tx, tc, tz = move(y, x, c, z)
                    src = ((y * NX + x) * NC + c) * NZ + z
                    dst = (((ty % NY) * NX + tx % NX) * NC + tc % NC) * NZ + tz % NZ
                    pairs.append((src, dst))
    return pairs


def send(array, move):
    return lax.ppermute(array, AXES, pairs_of(move))


def first_axis(array, by):
    return send(array, lambda y, x, c, z: (y, x + by, c, z) if c == 0 else (y + by, x, c, z))


def second_axis(array, by):
    return send(array, lambda y, x, c, z: (y + by, x, c, z) if c == 0 else (y, x + by, c, z))


def other_core(array):
    return send(array, lambda y, x, c, z: (y, x, 1 - c, z))


def along_z(array, by):
    return send(array, lambda y, x, c, z: (y, x, c, z + by))


def shifted(x, by):
    devices = lax.axis_size("section")
    pairs = [(i, i + by) for i in range(devices) if 0 <= i + by < devices]
    return lax.ppermute(x, "section", pairs)


def matmul(left, right):
    return jnp.dot(left, right, preferred_element_type=F32)


def contract(left, right, dims):
    return lax.dot_general(left, right, ((dims[:1], dims[1:]), ((), ())), preferred_element_type=F32)


def softmax_probs(query, *kv_refs):
    scores = jnp.concatenate([contract(query, ref[:, :HEAD_SIZE], (1, 1)) for ref in kv_refs], axis=1)
    scores = scores * (1.0 / math.sqrt(HEAD_SIZE))
    weights = jnp.exp(scores - jnp.max(scores, axis=-1, keepdims=True))
    return weights / jnp.sum(weights, axis=-1, keepdims=True)


def over_rows(left, start_col, *kv_refs):
    total, done = None, 0
    for ref in kv_refs:
        part = matmul(left[:, done : done + ref.shape[0]], ref[:, start_col : start_col + HEAD_SIZE])
        total = part if total is None else total + part
        done += ref.shape[0]
    return total


def on_vmem(kernel, shapes, *operands, place=None, far_in=(), far_out=(), scratch=()):
    vmem, left = pl.BlockSpec(memory_space=pltpu.VMEM), pl.BlockSpec(memory_space=pl.ANY)
    first = [] if place is None else [pl.BlockSpec(memory_space=pltpu.SMEM)]
    outs = [jax.ShapeDtypeStruct(*shape) for shape in shapes]
    held = sum(max(a.size, 8 * 128) * a.dtype.itemsize for a in (*operands, *outs))
    call = pl.pallas_call(
        kernel,
        out_shape=outs,
        in_specs=first + [left if i in far_in else vmem for i in range(len(operands))],
        out_specs=[left if i in far_out else vmem for i in range(len(shapes))],
        scratch_shapes=list(scratch),
        compiler_params=pltpu.CompilerParams(vmem_limit_bytes=held + 3 * 2**20),
        cost_estimate=pl.CostEstimate(flops=2 * 10**9, bytes_accessed=held, transcendentals=0),
    )
    return call(*([] if place is None else [place]), *operands)


def start(source, target, sem):
    copy = pltpu.make_async_copy(source, target, sem)
    copy.start()
    return copy


def stack_kernel(*refs):
    (*parts, out_ref), held, sems = refs[:-2], refs[-2], refs[-1]
    copies, start = [], 0
    for i, ref in enumerate(parts):
        at = pl.ds(start, ref.shape[0])
        into = pltpu.make_async_copy(ref, held.at[at], sems.at[i])
        copies.append((into, pltpu.make_async_copy(held.at[at], out_ref.at[at], sems.at[len(parts) + i])))
        start += ref.shape[0]
    for into, _ in copies:
        into.start()
    for into, out in copies:
        into.wait()
        out.start()
    for _, out in copies:
        out.wait()


def stack(*parts):
    shape = (sum(part.shape[0] for part in parts), parts[0].shape[1])
    hbm = pl.BlockSpec(memory_space=pl.ANY)
    return pl.pallas_call(
        stack_kernel,
        out_shape=jax.ShapeDtypeStruct(shape, parts[0].dtype),
        in_specs=[hbm] * len(parts),
        out_specs=hbm,
        scratch_shapes=[pltpu.VMEM(shape, parts[0].dtype), pltpu.SemaphoreType.DMA((2 * len(parts),))],
        cost_estimate=pl.CostEstimate(flops=1, bytes_accessed=1, transcendentals=0),
    )(*parts)


def heads_kernel(
    all_far, gain_far, wq_far, wo_far, kv_0, kv_1, kv_2, kv_3, d_key_far, d_value_far, factor_far, out_far,
    all_ref, gain_ref, wq_ref, wo_ref, kv_0_ref, kv_1_ref, kv_2_ref, kv_3_ref, d_key_ref, d_value_ref, factor_ref, out_ref,
    sems,
):
    kv_refs = (kv_0_ref, kv_1_ref, kv_2_ref, kv_3_ref)
    rows, cols = factor_ref.shape[0], out_ref.shape[2]
    width = all_ref.shape[1]
    first_copies, wq_copies = [], []
    for k in range(NZ):
        at = pl.ds(k * cols, cols)
        first_copies.append((
            start(all_far.at[:, at], all_ref.at[:, at], sems.at[0, k]),
            start(wo_far.at[:, at], wo_ref.at[:, at], sems.at[1, k]),
        ))
    gain_copy = start(gain_far, gain_ref, sems.at[3, 0])
    for k in range(NZ):
        at = pl.ds(k * cols, cols)
        wq_copies.append(start(wq_far.at[at], wq_ref.at[at], sems.at[2, k]))
    kv_copies = [start(far, ref, sems.at[3, 1 + i]) for i, (far, ref) in enumerate(zip((kv_0, kv_1, kv_2, kv_3), kv_refs))]

    squares = [jnp.zeros((rows, cols), F32) for _ in range(2)]
    d_att = jnp.zeros((rows, HEAD_SIZE), F32)
    for k in range(NZ):
        at = slice(k * cols, (k + 1) * cols)
        for copy in first_copies[k]:
            copy.wait()
        for block in range(2):
            wide = all_ref[block * rows : (block + 1) * rows, at].astype(F32)
            squares[block] = squares[block] + wide * wide
        d_att = d_att + contract(all_ref[2 * rows :, at], wo_ref[:, at], (1, 1))
    d_att = d_att.astype(BF)
    factors = []
    for block in range(2):
        mean = jnp.sum(squares[block], axis=-1, keepdims=True) * (1.0 / width)
        factors.append(lax.rsqrt(mean + 1e-06))
    factor_ref[...] = factors[1]
    out_copies = [start(factor_ref, factor_far, sems.at[3, 5])]
    gain_copy.wait()
    queries = [jnp.zeros((rows, HEAD_SIZE), F32) for _ in range(2)]
    for k in range(NZ):
        at = slice(k * cols, (k + 1) * cols)
        wq_copies[k].wait()
        for block in range(2):
            normed = all_ref[block * rows : (block + 1) * rows, at].astype(F32) * factors[block] * gain_ref[:, at]
            queries[block] = queries[block] + matmul(normed.astype(BF), wq_ref[at, :])

    for copy in kv_copies:
        copy.wait()
    query = queries[1].astype(BF)
    probs = softmax_probs(query, *kv_refs)
    d_probs = jnp.concatenate([contract(d_att, ref[:, HEAD_SIZE:], (1, 1)) for ref in kv_refs], axis=1)
    inner = jnp.sum(probs * d_probs, axis=-1, keepdims=True)
    d_score = (probs * (d_probs - inner) * (1.0 / math.sqrt(HEAD_SIZE))).astype(BF)
    d_key_ref[...] = contract(d_score, query, (0, 0)).astype(BF)
    out_copies.append(start(d_key_ref, d_key_far, sems.at[3, 6]))
    d_value_ref[...] = contract(probs.astype(BF), d_att, (0, 0)).astype(BF)
    out_copies.append(start(d_value_ref, d_value_far, sems.at[3, 7]))
    d_query = over_rows(d_score, 0, *kv_refs).astype(BF)
    extra_rows = out_ref.shape[1] - 2 * rows
    sums = lax.dot_general(
        jnp.ones((extra_rows, HEAD_SIZE), F32),
        d_query.astype(F32) * queries[1],
        (((1,), (1,)), ((), ())),
        precision=lax.Precision.HIGHEST,
        preferred_element_type=F32,
    )
    sums = jnp.concatenate([sums, jnp.zeros((extra_rows, cols - rows), F32)], axis=1).astype(BF)

    probs = softmax_probs(queries[0].astype(BF), *kv_refs).astype(BF)
    attended = over_rows(probs, HEAD_SIZE, *kv_refs).astype(BF)
    for k in range(NZ):
        at = slice(k * cols, (k + 1) * cols)
        out_ref[k, :rows] = contract(d_query, wq_ref[at, :], (1, 1)).astype(BF)
        out_ref[k, rows : 2 * rows] = matmul(attended, wo_ref[:, at]).astype(BF)
        out_ref[k, 2 * rows :] = sums
        out_copies.append(start(out_ref.at[k], out_far.at[k], sems.at[4, k]))
    for copy in out_copies:
        copy.wait()


def memory_part(d_key, d_value, wk_ref, wv_ref, out_refs, *added):
    width, tile = wk_ref.shape[0], 512

    def tile_of(refs, k):
        ref = refs[k * tile * len(refs) // width]
        at = k * tile % ref.shape[1]
        return ref, slice(at, at + tile)

    for k in range(width // tile):
        at = slice(k * tile, (k + 1) * tile)
        part = contract(d_key, wk_ref[at, :], (1, 1)) + contract(d_value, wv_ref[at, :], (1, 1))
        for refs in added:
            ref, cols = tile_of(refs, k)
            part = part + ref[:, cols].astype(F32)
        ref, cols = tile_of(out_refs, k)
        ref[:, cols] = part.astype(ref.dtype)


def finish_kernel(place_ref, sums_ref, x_ref, h_ref, g_ref, factor_ref, gain_ref, layer_ref, d_in_ref):
    rows, cols = x_ref.shape
    layer_ref[...] = (x_ref[...].astype(F32) + sums_ref[rows : 2 * rows].astype(F32)).astype(BF)
    factor = factor_ref[...]
    at = pl.multiple_of(place_ref[0] * cols, cols)
    gain = gain_ref[:, pl.ds(at, cols)]
    eye = lax.broadcasted_iota(jnp.int32, (rows, rows), 0) == lax.broadcasted_iota(jnp.int32, (rows, rows), 1)
    inner = contract(jnp.where(eye, 1.0, 0.0).astype(BF), sums_ref[2 * rows :, :rows], (1, 1))[:, :1]
    inner = inner / factor * (1.0 / (NZ * cols))
    d_in = g_ref[...].astype(F32) + factor * gain * sums_ref[:rows].astype(F32)
    d_in_ref[...] = (d_in - h_ref[...].astype(F32) * (factor * factor * factor * inner)).astype(BF)


def cross_kernel(blocks, d_key_ref, d_value_ref, wk_ref, wv_ref, *refs):
    for i, ref in zip(blocks, refs[-len(blocks) :]):
        at = slice((4 + i) * ref.shape[0], (5 + i) * ref.shape[0])
        memory_part(d_key_ref[at], d_value_ref[at], wk_ref, wv_ref, [ref])


def halves_kernel(columns_from, d_key_ref, d_value_ref, wk_ref, wv_ref, *refs):
    rows = refs[-1].shape[0]
    at = slice(columns_from * rows, (columns_from + 1) * rows)
    memory_part(d_key_ref[at], d_value_ref[at], wk_ref, wv_ref, refs[-2:], refs[:-2])


def middle_kernel(d_key_ref, d_value_ref, wk_ref, wv_ref, low_ref, high_ref, out_low, out_high):
    rows, cols = out_low.shape
    width, tile = wk_ref.shape[0], 512
    for block, ref, arrived, start in ((1, out_low, low_ref, cols), (2, out_high, high_ref, 0)):
        rows_at = slice(block * rows, (block + 1) * rows)
        for k in range(cols // tile):
            at = slice(start + k * tile, start + (k + 1) * tile)
            part = contract(d_key_ref[rows_at], wk_ref[at, :], (1, 1))
            part = part + contract(d_value_ref[rows_at], wv_ref[at, :], (1, 1))
            ref[:, k * tile : (k + 1) * tile] = (part + arrived[:, at].astype(F32)).astype(ref.dtype)


def edge_kernel(d_key_ref, d_value_ref, wk_ref, wv_ref, low_ref, high_ref, add_low, add_high, out_low, out_high):
    rows, cols = out_low.shape
    width, tile = wk_ref.shape[0], 512
    for block, ref, arrived, add, start in ((1, out_low, low_ref, add_low, 0), (2, out_high, high_ref, add_high, cols)):
        rows_at = slice(block * rows, (block + 1) * rows)
        for k in range(cols // tile):
            at = slice(start + k * tile, start + (k + 1) * tile)
            here = slice(k * tile, (k + 1) * tile)
            part = contract(d_key_ref[rows_at], wk_ref[at, :], (1, 1))
            part = part + contract(d_value_ref[rows_at], wv_ref[at, :], (1, 1))
            part = part + arrived[:, at].astype(F32) + add[:, here].astype(F32)
            ref[:, here] = part.astype(ref.dtype)


def near_kernel(
    d_key_ref, d_value_ref, wk_ref, wv_ref, arrived_ref, low_a, low_b, high_a, high_b, mine_ref, *wires
):
    mine, rows = mine_ref.shape[0], arrived_ref.shape[0]
    width, tile = wk_ref.shape[0], 512
    cols = low_a.shape[1]
    for k in range(width // tile):
        at = slice(k * tile, (k + 1) * tile)
        part = contract(d_key_ref[:rows], wk_ref[at, :], (1, 1)) + contract(d_value_ref[:rows], wv_ref[at, :], (1, 1))
        low, high = (low_a, high_a) if k * tile < cols else (low_b, high_b)
        here = slice(k * tile % cols, k * tile % cols + tile)
        part = part + arrived_ref[:, at].astype(F32) + low[:, here].astype(F32) + high[:, here].astype(F32)
        for i, ref in enumerate((mine_ref, *wires)):
            ref[:, at] = part[i * mine : (i + 1) * mine].astype(ref.dtype)


def assemble_kernel(a_ref, b_ref, c_ref, d_ref, first_ref, second_ref, near_ref):
    mine, cols = a_ref.shape[0], first_ref.shape[1]
    for i, ref in enumerate((a_ref, b_ref, c_ref, d_ref)):
        at = slice(i * mine, (i + 1) * mine)
        first_ref[at] = ref[:, :cols]
        second_ref[at] = ref[:, cols:]
        near_ref[at] = ref[...]


def keys_kernel(count, *refs):
    pieces, wk_ref, wv_ref, out_ref = refs[:count], refs[count], refs[count + 1], refs[-1]
    rows, width, tile = pieces[0].shape[0], wk_ref.shape[0], 1024
    blocks = []
    while pieces:
        count = width // pieces[0].shape[1]
        blocks.append(pieces[:count])
        pieces = pieces[count:]
    for i, block in enumerate(blocks):
        for w_ref, at in ((wk_ref, 0), (wv_ref, HEAD_SIZE)):
            total = jnp.zeros((rows, HEAD_SIZE), F32)
            for k in range(width // tile):
                ref = block[k * tile * len(block) // width]
                here = k * tile % ref.shape[1]
                total = total + matmul(ref[:, here : here + tile], w_ref[k * tile : (k + 1) * tile, :])
            out_ref[i * rows : (i + 1) * rows, at : at + HEAD_SIZE] = total.astype(BF)


def spread_kernel(mine_ref, a_ref, b_ref, c_ref, block_ref, grad_ref, out_ref):
    rows, cols = mine_ref.shape[0], out_ref.shape[1]
    for k in range(NZ):
        at = slice(k * cols, (k + 1) * cols)
        total = mine_ref[:, at] + a_ref[:, at].astype(F32) + b_ref[:, at].astype(F32) + c_ref[:, at].astype(F32)
        out_ref[k * rows : (k + 1) * rows] = total.astype(BF)


def total_kernel(parts_ref, out_ref):
    rows = out_ref.shape[0]
    total = parts_ref[:rows].astype(F32)
    for k in range(1, NZ):
        total = total + parts_ref[k * rows : (k + 1) * rows].astype(F32)
    out_ref[...] = total


def body(block_in, saved_in, block_grad, memory, norm_gain, w_query, w_key, w_value, w_out):
    rows, cols = block_in.shape
    width, size = w_query.shape[1:]
    at_z = lax.axis_index("tensor").reshape(1)

    gathered = lax.all_gather(stack(block_in, saved_in, block_grad), "tensor", axis=1, tiled=True)
    wq, wk, wv, wo = w_query[0], w_key[0], w_value[0], w_out[0]

    mem = NY * NX * NC * memory.shape[0]
    quarter = mem // 8
    half = ((quarter, width // 2), BF)
    near_a, near_b, near = on_vmem(
        assemble_kernel, [half] * 2 + [((quarter, width), BF)], memory, first_axis(memory, 1), first_axis(memory, -1), first_axis(memory, 2)
    )
    low_a, high_b = second_axis(near_a, 1), second_axis(near_b, -1)
    low_b, high_a = second_axis(near_b, 1), second_axis(near_a, -1)
    far_a, far_b = second_axis(low_a, 1), second_axis(high_b, -1)

    near_sent, low_a, high_b = lax.optimization_barrier((near, low_a, high_b))
    others = [other_core(piece) for piece in (near_sent, low_a, low_b, high_a, high_b)]

    def keys_of(*pieces):
        blocks = sum(piece.shape[1] for piece in pieces) // width
        kernel = functools.partial(keys_kernel, len(pieces))
        return on_vmem(kernel, [((blocks * quarter, 2 * size), BF)], *pieces, wk, wv)[0]

    kv = (
        keys_of(near, low_a, low_b, high_a, high_b),
        keys_of(far_a, far_b),
        keys_of(*others),
        keys_of(other_core(far_a), other_core(far_b)),
    )

    ins = (gathered, norm_gain, wq, wo, *kv)
    outs = [((mem, size), BF), ((mem, size), BF), ((rows, 1), F32), ((NZ, 2 * rows + 16, cols), BF)]
    far = pl.BlockSpec(memory_space=pltpu.HBM)
    d_key, d_value, factor_h, sent = pl.pallas_call(
        heads_kernel,
        out_shape=[jax.ShapeDtypeStruct(*out) for out in outs],
        in_specs=[far] * len(ins),
        out_specs=[far] * len(outs),
        scratch_shapes=[pltpu.VMEM(a.shape, a.dtype) for a in ins]
        + [pltpu.VMEM(*out) for out in outs]
        + [pltpu.SemaphoreType.DMA((5, NZ))],
        compiler_params=pltpu.CompilerParams(vmem_limit_bytes=60 * 2**20),
        cost_estimate=pl.CostEstimate(flops=4 * 10**9, bytes_accessed=12 * 2**20, transcendentals=0),
    )(*ins)
    summed = lax.psum_scatter(sent, "tensor", scatter_dimension=0, tiled=True)[0]
    layer_out, d_in = on_vmem(
        finish_kernel, [((rows, cols), BF)] * 2, summed, block_in, saved_in, block_grad, factor_h, norm_gain,
        place=at_z,
    )
    next_block, prev_grad = shifted(layer_out, 1), shifted(d_in, -1)

    mine = memory.shape[0]
    own = (d_key, d_value, wk, wv)
    whole = ((quarter, width), BF)

    def cross(blocks, *after):
        kernel = functools.partial(cross_kernel, blocks)
        return [other_core(block) for block in on_vmem(kernel, [whole] * len(blocks), *own, *after)]

    (far,) = cross((3,))
    low, high = cross((1, 2))
    far_a, far_b = on_vmem(functools.partial(halves_kernel, 3), [half] * 2, *own, far)
    (near,) = cross((0,), far_a)
    low_b, high_a = on_vmem(middle_kernel, [half] * 2, *own, low, high)
    back_low_b, back_high_a = second_axis(low_b, -1), second_axis(high_a, 1)
    low_a, high_b = on_vmem(
        edge_kernel, [half] * 2, *own, low, high, second_axis(far_a, -1), second_axis(far_b, 1)
    )
    back_low_a, back_high_b = second_axis(low_a, -1), second_axis(high_b, 1)
    t_mine, *wires = on_vmem(
        near_kernel,
        [((mine, width), F32)] + [((mine, width), BF)] * 3,
        *own, near, back_low_a, back_low_b, back_high_a, back_high_b,
    )
    arrived = [first_axis(wires[0], -1), first_axis(wires[1], 1), first_axis(wires[2], 2)]
    (spread,) = on_vmem(spread_kernel, [((NZ * mine, cols), BF)], t_mine, *arrived, layer_out, d_in)
    parts = lax.all_to_all(spread, "tensor", 0, 0, tiled=True)
    (memory_grad,) = on_vmem(total_kernel, [((mine, cols), F32)], parts)
    return next_block, prev_grad, memory_grad


def solution(mesh):
    in_specs = (
        P("section", "tensor"),
        P("section", "tensor"),
        P("section", "tensor"),
        P("section", None),
        P("section", None),
        P("section", None, "tensor"),
        P("section", None, "tensor"),
        P("section", None, "tensor"),
        P("section", "tensor", None),
    )
    out_specs = (P("section", "tensor"), P("section", "tensor"), P("section", "tensor"))
    return jax.shard_map(body, mesh=mesh, in_specs=in_specs, out_specs=out_specs, check_vma=False)
```

```python
import functools
import math

import jax
import jax.numpy as jnp
from jax import lax
from jax.experimental import pallas as pl
from jax.experimental.pallas import tpu as pltpu
from jax.sharding import PartitionSpec as P

HEAD_SIZE = 256
NY, NX, NC, NZ = 4, 4, 2, 8
AXES = ("section", "tensor")
BF = jnp.bfloat16
F32 = jnp.float32


def pairs_of(move):
    pairs = []
    for y in range(NY):
        for x in range(NX):
            for c in range(NC):
                for z in range(NZ):
                    ty, tx, tc, tz = move(y, x, c, z)
                    src = ((y * NX + x) * NC + c) * NZ + z
                    dst = (((ty % NY) * NX + tx % NX) * NC + tc % NC) * NZ + tz % NZ
                    pairs.append((src, dst))
    return pairs


def send(array, move):
    return lax.ppermute(array, AXES, pairs_of(move))


def first_axis(array, by):
    return send(array, lambda y, x, c, z: (y, x + by, c, z) if c == 0 else (y + by, x, c, z))


def second_axis(array, by):
    return send(array, lambda y, x, c, z: (y + by, x, c, z) if c == 0 else (y, x + by, c, z))


def other_core(array):
    return send(array, lambda y, x, c, z: (y, x, 1 - c, z))


def along_z(array, by):
    return send(array, lambda y, x, c, z: (y, x, c, z + by))


def shifted(x, by):
    devices = lax.axis_size("section")
    pairs = [(i, i + by) for i in range(devices) if 0 <= i + by < devices]
    return lax.ppermute(x, "section", pairs)


def matmul(left, right):
    return jnp.dot(left, right, preferred_element_type=F32)


def contract(left, right, dims):
    return lax.dot_general(left, right, ((dims[:1], dims[1:]), ((), ())), preferred_element_type=F32)


def softmax_probs(query, *kv_refs):
    scores = jnp.concatenate([contract(query, ref[:, :HEAD_SIZE], (1, 1)) for ref in kv_refs], axis=1)
    scores = scores * (1.0 / math.sqrt(HEAD_SIZE))
    weights = jnp.exp(scores - jnp.max(scores, axis=-1, keepdims=True))
    return weights / jnp.sum(weights, axis=-1, keepdims=True)


def over_rows(left, start_col, *kv_refs):
    total, done = None, 0
    for ref in kv_refs:
        part = matmul(left[:, done : done + ref.shape[0]], ref[:, start_col : start_col + HEAD_SIZE])
        total = part if total is None else total + part
        done += ref.shape[0]
    return total


def on_vmem(kernel, shapes, *operands, place=None, far_in=(), far_out=(), scratch=()):
    vmem, left = pl.BlockSpec(memory_space=pltpu.VMEM), pl.BlockSpec(memory_space=pl.ANY)
    first = [] if place is None else [pl.BlockSpec(memory_space=pltpu.SMEM)]
    outs = [jax.ShapeDtypeStruct(*shape) for shape in shapes]
    held = sum(max(a.size, 8 * 128) * a.dtype.itemsize for a in (*operands, *outs))
    call = pl.pallas_call(
        kernel,
        out_shape=outs,
        in_specs=first + [left if i in far_in else vmem for i in range(len(operands))],
        out_specs=[left if i in far_out else vmem for i in range(len(shapes))],
        scratch_shapes=list(scratch),
        compiler_params=pltpu.CompilerParams(vmem_limit_bytes=held + 3 * 2**20),
        cost_estimate=pl.CostEstimate(flops=2 * 10**9, bytes_accessed=held, transcendentals=0),
    )
    return call(*([] if place is None else [place]), *operands)


def start(source, target, sem):
    copy = pltpu.make_async_copy(source, target, sem)
    copy.start()
    return copy


def stack_kernel(*refs):
    (*parts, out_ref), held, sems = refs[:-2], refs[-2], refs[-1]
    copies, start = [], 0
    for i, ref in enumerate(parts):
        at = pl.ds(start, ref.shape[0])
        into = pltpu.make_async_copy(ref, held.at[at], sems.at[i])
        copies.append((into, pltpu.make_async_copy(held.at[at], out_ref.at[at], sems.at[len(parts) + i])))
        start += ref.shape[0]
    for into, _ in copies:
        into.start()
    for into, out in copies:
        into.wait()
        out.start()
    for _, out in copies:
        out.wait()


def stack(*parts):
    shape = (sum(part.shape[0] for part in parts), parts[0].shape[1])
    hbm = pl.BlockSpec(memory_space=pl.ANY)
    return pl.pallas_call(
        stack_kernel,
        out_shape=jax.ShapeDtypeStruct(shape, parts[0].dtype),
        in_specs=[hbm] * len(parts),
        out_specs=hbm,
        scratch_shapes=[pltpu.VMEM(shape, parts[0].dtype), pltpu.SemaphoreType.DMA((2 * len(parts),))],
        cost_estimate=pl.CostEstimate(flops=1, bytes_accessed=1, transcendentals=0),
    )(*parts)


def heads_kernel(
    all_far, gain_far, wq_far, wo_far, kv_0, kv_1, kv_2, kv_3, d_key_far, d_value_far, out_far,
    all_ref, gain_ref, wq_ref, wo_ref, kv_0_ref, kv_1_ref, kv_2_ref, kv_3_ref, d_key_ref, d_value_ref, out_ref,
    sems,
):
    kv_refs = (kv_0_ref, kv_1_ref, kv_2_ref, kv_3_ref)
    rows, cols = all_ref.shape[0] // 3, out_ref.shape[2]
    width = all_ref.shape[1]
    first_copies, wq_copies = [], []
    for k in range(NZ):
        at = pl.ds(k * cols, cols)
        first_copies.append((
            start(all_far.at[:, at], all_ref.at[:, at], sems.at[0, k]),
            start(wo_far.at[:, at], wo_ref.at[:, at], sems.at[1, k]),
        ))
    gain_copy = start(gain_far, gain_ref, sems.at[3, 0])
    for k in range(NZ):
        at = pl.ds(k * cols, cols)
        wq_copies.append(start(wq_far.at[at], wq_ref.at[at], sems.at[2, k]))
    kv_copies = [start(far, ref, sems.at[3, 1 + i]) for i, (far, ref) in enumerate(zip((kv_0, kv_1, kv_2, kv_3), kv_refs))]

    squares = [jnp.zeros((rows, cols), F32) for _ in range(2)]
    d_att = jnp.zeros((rows, HEAD_SIZE), F32)
    for k in range(NZ):
        at = slice(k * cols, (k + 1) * cols)
        for copy in first_copies[k]:
            copy.wait()
        for block in range(2):
            wide = all_ref[block * rows : (block + 1) * rows, at].astype(F32)
            squares[block] = squares[block] + wide * wide
        d_att = d_att + contract(all_ref[2 * rows :, at], wo_ref[:, at], (1, 1))
    d_att = d_att.astype(BF)
    factors = []
    for block in range(2):
        mean = jnp.sum(squares[block], axis=-1, keepdims=True) * (1.0 / width)
        factors.append(lax.rsqrt(mean + 1e-06))
    out_copies = []
    gain_copy.wait()
    queries = [jnp.zeros((rows, HEAD_SIZE), F32) for _ in range(2)]
    for k in range(NZ):
        at = slice(k * cols, (k + 1) * cols)
        wq_copies[k].wait()
        for block in range(2):
            normed = all_ref[block * rows : (block + 1) * rows, at].astype(F32) * factors[block] * gain_ref[:, at]
            queries[block] = queries[block] + matmul(normed.astype(BF), wq_ref[at, :])

    for copy in kv_copies:
        copy.wait()
    query = queries[1].astype(BF)
    probs = softmax_probs(query, *kv_refs)
    d_probs = jnp.concatenate([contract(d_att, ref[:, HEAD_SIZE:], (1, 1)) for ref in kv_refs], axis=1)
    inner = jnp.sum(probs * d_probs, axis=-1, keepdims=True)
    d_score = (probs * (d_probs - inner) * (1.0 / math.sqrt(HEAD_SIZE))).astype(BF)
    d_key_ref[...] = contract(d_score, query, (0, 0)).astype(BF)
    out_copies.append(start(d_key_ref, d_key_far, sems.at[3, 6]))
    d_value_ref[...] = contract(probs.astype(BF), d_att, (0, 0)).astype(BF)
    out_copies.append(start(d_value_ref, d_value_far, sems.at[3, 7]))
    d_query = over_rows(d_score, 0, *kv_refs).astype(BF)
    extra_rows = out_ref.shape[1] - 2 * rows
    sums = lax.dot_general(
        jnp.ones((extra_rows, HEAD_SIZE), F32),
        d_query.astype(F32) * queries[1] * (factors[1] * factors[1] * (1.0 / width)),
        (((1,), (1,)), ((), ())),
        precision=lax.Precision.HIGHEST,
        preferred_element_type=F32,
    )
    sums = jnp.concatenate([sums, jnp.zeros((extra_rows, cols - rows), F32)], axis=1).astype(BF)

    probs = softmax_probs(queries[0].astype(BF), *kv_refs).astype(BF)
    attended = over_rows(probs, HEAD_SIZE, *kv_refs).astype(BF)
    for k in range(NZ):
        at = slice(k * cols, (k + 1) * cols)
        out_ref[k, :rows] = (contract(d_query, wq_ref[at, :], (1, 1)) * factors[1]).astype(BF)
        out_ref[k, rows : 2 * rows] = matmul(attended, wo_ref[:, at]).astype(BF)
        out_ref[k, 2 * rows :] = sums
        out_copies.append(start(out_ref.at[k], out_far.at[k], sems.at[4, k]))
    for copy in out_copies:
        copy.wait()


def memory_part(d_key, d_value, wk_ref, wv_ref, out_refs, *added):
    width, tile = wk_ref.shape[0], 512

    def tile_of(refs, k):
        ref = refs[k * tile * len(refs) // width]
        at = k * tile % ref.shape[1]
        return ref, slice(at, at + tile)

    for k in range(width // tile):
        at = slice(k * tile, (k + 1) * tile)
        part = contract(d_key, wk_ref[at, :], (1, 1)) + contract(d_value, wv_ref[at, :], (1, 1))
        for refs in added:
            ref, cols = tile_of(refs, k)
            part = part + ref[:, cols].astype(F32)
        ref, cols = tile_of(out_refs, k)
        ref[:, cols] = part.astype(ref.dtype)


def finish_kernel(place_ref, sums_ref, x_ref, h_ref, g_ref, gain_ref, layer_ref, d_in_ref):
    rows, cols = x_ref.shape
    layer_ref[...] = (x_ref[...].astype(F32) + sums_ref[rows : 2 * rows].astype(F32)).astype(BF)
    at = pl.multiple_of(place_ref[0] * cols, cols)
    gain = gain_ref[:, pl.ds(at, cols)]
    eye = lax.broadcasted_iota(jnp.int32, (rows, rows), 0) == lax.broadcasted_iota(jnp.int32, (rows, rows), 1)
    inner = contract(jnp.where(eye, 1.0, 0.0).astype(BF), sums_ref[2 * rows :, :rows], (1, 1))[:, :1]
    d_in = g_ref[...].astype(F32) + gain * sums_ref[:rows].astype(F32)
    d_in_ref[...] = (d_in - h_ref[...].astype(F32) * inner).astype(BF)


def cross_kernel(blocks, d_key_ref, d_value_ref, wk_ref, wv_ref, *refs):
    for i, ref in zip(blocks, refs[-len(blocks) :]):
        at = slice((4 + i) * ref.shape[0], (5 + i) * ref.shape[0])
        memory_part(d_key_ref[at], d_value_ref[at], wk_ref, wv_ref, [ref])


def halves_kernel(columns_from, d_key_ref, d_value_ref, wk_ref, wv_ref, *refs):
    rows = refs[-1].shape[0]
    at = slice(columns_from * rows, (columns_from + 1) * rows)
    memory_part(d_key_ref[at], d_value_ref[at], wk_ref, wv_ref, refs[-2:], refs[:-2])


def middle_kernel(d_key_ref, d_value_ref, wk_ref, wv_ref, low_ref, high_ref, out_low, out_high):
    rows, cols = out_low.shape
    width, tile = wk_ref.shape[0], 512
    for block, ref, arrived, start in ((1, out_low, low_ref, cols), (2, out_high, high_ref, 0)):
        rows_at = slice(block * rows, (block + 1) * rows)
        for k in range(cols // tile):
            at = slice(start + k * tile, start + (k + 1) * tile)
            part = contract(d_key_ref[rows_at], wk_ref[at, :], (1, 1))
            part = part + contract(d_value_ref[rows_at], wv_ref[at, :], (1, 1))
            ref[:, k * tile : (k + 1) * tile] = (part + arrived[:, at].astype(F32)).astype(ref.dtype)


def edge_kernel(d_key_ref, d_value_ref, wk_ref, wv_ref, low_ref, high_ref, add_low, add_high, out_low, out_high):
    rows, cols = out_low.shape
    width, tile = wk_ref.shape[0], 512
    for block, ref, arrived, add, start in ((1, out_low, low_ref, add_low, 0), (2, out_high, high_ref, add_high, cols)):
        rows_at = slice(block * rows, (block + 1) * rows)
        for k in range(cols // tile):
            at = slice(start + k * tile, start + (k + 1) * tile)
            here = slice(k * tile, (k + 1) * tile)
            part = contract(d_key_ref[rows_at], wk_ref[at, :], (1, 1))
            part = part + contract(d_value_ref[rows_at], wv_ref[at, :], (1, 1))
            part = part + arrived[:, at].astype(F32) + add[:, here].astype(F32)
            ref[:, here] = part.astype(ref.dtype)


def near_kernel(d_key_ref, d_value_ref, wk_ref, wv_ref, arrived_ref, out_ref):
    rows = arrived_ref.shape[0]
    memory_part(d_key_ref[:rows], d_value_ref[:rows], wk_ref, wv_ref, [out_ref], [arrived_ref])


def collect_kernel(near_ref, low_a, low_b, high_a, high_b, mine_ref, *wires):
    mine, cols, tile = mine_ref.shape[0], low_a.shape[1], 512
    for k in range(near_ref.shape[1] // tile):
        at = slice(k * tile, (k + 1) * tile)
        low, high = (low_a, high_a) if k * tile < cols else (low_b, high_b)
        here = slice(k * tile % cols, k * tile % cols + tile)
        total = near_ref[:, at] + low[:, here].astype(F32) + high[:, here].astype(F32)
        for i, ref in enumerate((mine_ref, *wires)):
            ref[:, at] = total[i * mine : (i + 1) * mine].astype(ref.dtype)


def assemble_kernel(a_ref, b_ref, c_ref, d_ref, first_ref, second_ref, near_ref):
    mine, cols = a_ref.shape[0], first_ref.shape[1]
    for i, ref in enumerate((a_ref, b_ref, c_ref, d_ref)):
        at = slice(i * mine, (i + 1) * mine)
        first_ref[at] = ref[:, :cols]
        second_ref[at] = ref[:, cols:]
        near_ref[at] = ref[...]


def keys_kernel(count, *refs):
    pieces, wk_ref, wv_ref, out_ref = refs[:count], refs[count], refs[count + 1], refs[-1]
    rows, width, tile = pieces[0].shape[0], wk_ref.shape[0], 1024
    blocks = []
    while pieces:
        count = width // pieces[0].shape[1]
        blocks.append(pieces[:count])
        pieces = pieces[count:]
    for i, block in enumerate(blocks):
        for w_ref, at in ((wk_ref, 0), (wv_ref, HEAD_SIZE)):
            total = jnp.zeros((rows, HEAD_SIZE), F32)
            for k in range(width // tile):
                ref = block[k * tile * len(block) // width]
                here = k * tile % ref.shape[1]
                total = total + matmul(ref[:, here : here + tile], w_ref[k * tile : (k + 1) * tile, :])
            out_ref[i * rows : (i + 1) * rows, at : at + HEAD_SIZE] = total.astype(BF)


def spread_kernel(mine_ref, a_ref, b_ref, c_ref, block_ref, grad_ref, out_ref):
    rows, cols = mine_ref.shape[0], out_ref.shape[1]
    for k in range(NZ):
        at = slice(k * cols, (k + 1) * cols)
        total = mine_ref[:, at] + a_ref[:, at].astype(F32) + b_ref[:, at].astype(F32) + c_ref[:, at].astype(F32)
        out_ref[k * rows : (k + 1) * rows] = total.astype(BF)


def total_kernel(parts_ref, block_ref, grad_ref, out_ref, block_out, grad_out):
    rows = out_ref.shape[0]
    total = parts_ref[:rows].astype(F32)
    for k in range(1, NZ):
        total = total + parts_ref[k * rows : (k + 1) * rows].astype(F32)
    out_ref[...] = total
    block_out[...] = block_ref[...]
    grad_out[...] = grad_ref[...]


def body(block_in, saved_in, block_grad, memory, norm_gain, w_query, w_key, w_value, w_out):
    rows, cols = block_in.shape
    width, size = w_query.shape[1:]
    at_z = lax.axis_index("tensor").reshape(1)

    gathered = lax.all_gather(stack(block_in, saved_in, block_grad), "tensor", axis=1, tiled=True)
    wq, wk, wv, wo = w_query[0], w_key[0], w_value[0], w_out[0]

    mem = NY * NX * NC * memory.shape[0]
    quarter = mem // 8
    half = ((quarter, width // 2), BF)
    near_a, near_b, near = on_vmem(
        assemble_kernel, [half] * 2 + [((quarter, width), BF)], memory, first_axis(memory, 1), first_axis(memory, -1), first_axis(memory, 2)
    )
    low_a, high_b = second_axis(near_a, 1), second_axis(near_b, -1)
    low_b, high_a = second_axis(near_b, 1), second_axis(near_a, -1)
    far_a, far_b = second_axis(low_a, 1), second_axis(high_b, -1)

    near_sent, low_a, high_b = lax.optimization_barrier((near, low_a, high_b))
    others = [other_core(piece) for piece in (near_sent, low_a, low_b, high_a, high_b)]

    def keys_of(*pieces):
        blocks = sum(piece.shape[1] for piece in pieces) // width
        kernel = functools.partial(keys_kernel, len(pieces))
        return on_vmem(kernel, [((blocks * quarter, 2 * size), BF)], *pieces, wk, wv)[0]

    kv = (
        keys_of(near, low_a, low_b, high_a, high_b),
        keys_of(far_a, far_b),
        keys_of(*others),
        keys_of(other_core(far_a), other_core(far_b)),
    )

    ins = (gathered, norm_gain, wq, wo, *kv)
    outs = [((mem, size), BF), ((mem, size), BF), ((NZ, 2 * rows + 16, cols), BF)]
    far = pl.BlockSpec(memory_space=pltpu.HBM)
    d_key, d_value, sent = pl.pallas_call(
        heads_kernel,
        out_shape=[jax.ShapeDtypeStruct(*out) for out in outs],
        in_specs=[far] * len(ins),
        out_specs=[far] * len(outs),
        scratch_shapes=[pltpu.VMEM(a.shape, a.dtype) for a in ins]
        + [pltpu.VMEM(*out) for out in outs]
        + [pltpu.SemaphoreType.DMA((5, NZ))],
        compiler_params=pltpu.CompilerParams(vmem_limit_bytes=60 * 2**20),
        cost_estimate=pl.CostEstimate(flops=4 * 10**9, bytes_accessed=12 * 2**20, transcendentals=0),
    )(*ins)
    summed = lax.psum_scatter(sent, "tensor", scatter_dimension=0, tiled=True)[0]
    layer_out, d_in = on_vmem(
        finish_kernel, [((rows, cols), BF)] * 2, summed, block_in, saved_in, block_grad, norm_gain,
        place=at_z,
    )
    next_block, prev_grad = shifted(layer_out, 1), shifted(d_in, -1)

    mine = memory.shape[0]
    own = (d_key, d_value, wk, wv)
    whole = ((quarter, width), BF)

    def cross(blocks, *after):
        kernel = functools.partial(cross_kernel, blocks)
        return [other_core(block) for block in on_vmem(kernel, [whole] * len(blocks), *own, *after)]

    (far,) = cross((3,))
    low, high = cross((1, 2))
    far_a, far_b = on_vmem(functools.partial(halves_kernel, 3), [half] * 2, *own, far)
    (near,) = cross((0,), far_a)
    low_b, high_a = on_vmem(middle_kernel, [half] * 2, *own, low, high)
    back_low_b, back_high_a = second_axis(low_b, -1), second_axis(high_a, 1)
    low_a, high_b = on_vmem(
        edge_kernel, [half] * 2, *own, low, high, second_axis(far_a, -1), second_axis(far_b, 1)
    )
    back_low_a, back_high_b = second_axis(low_a, -1), second_axis(high_b, 1)
    (near,) = on_vmem(near_kernel, [((quarter, width), F32)], *own, near)
    t_mine, *wires = on_vmem(
        collect_kernel,
        [((mine, width), F32)] + [((mine, width), BF)] * 3,
        near, back_low_a, back_low_b, back_high_a, back_high_b,
    )
    arrived = [first_axis(wires[0], -1), first_axis(wires[1], 1), first_axis(wires[2], 2)]
    (spread,) = on_vmem(spread_kernel, [((NZ * mine, cols), BF)], t_mine, *arrived, layer_out, d_in)
    parts = lax.all_to_all(spread, "tensor", 0, 0, tiled=True)
    memory_grad, next_block, prev_grad = on_vmem(
        total_kernel, [((mine, cols), F32)] + [((rows, cols), BF)] * 2, parts, next_block, prev_grad
    )
    return next_block, prev_grad, memory_grad


def solution(mesh):
    in_specs = (
        P("section", "tensor"),
        P("section", "tensor"),
        P("section", "tensor"),
        P("section", None),
        P("section", None),
        P("section", None, "tensor"),
        P("section", None, "tensor"),
        P("section", None, "tensor"),
        P("section", "tensor", None),
    )
    out_specs = (P("section", "tensor"), P("section", "tensor"), P("section", "tensor"))
    return jax.shard_map(body, mesh=mesh, in_specs=in_specs, out_specs=out_specs, check_vma=False)
```

```python
import functools
import math

import jax
import jax.numpy as jnp
from jax import lax
from jax.experimental import pallas as pl
from jax.experimental.pallas import tpu as pltpu
from jax.sharding import PartitionSpec as P

HEAD_SIZE = 256
NY, NX, NC, NZ = 4, 4, 2, 8
AXES = ("section", "tensor")
BF = jnp.bfloat16
F32 = jnp.float32


def pairs_of(move):
    pairs = []
    for y in range(NY):
        for x in range(NX):
            for c in range(NC):
                for z in range(NZ):
                    ty, tx, tc, tz = move(y, x, c, z)
                    src = ((y * NX + x) * NC + c) * NZ + z
                    dst = (((ty % NY) * NX + tx % NX) * NC + tc % NC) * NZ + tz % NZ
                    pairs.append((src, dst))
    return pairs


def send(array, move):
    return lax.ppermute(array, AXES, pairs_of(move))


def first_axis(array, by):
    return send(array, lambda y, x, c, z: (y, x + by, c, z) if c == 0 else (y + by, x, c, z))


def second_axis(array, by):
    return send(array, lambda y, x, c, z: (y + by, x, c, z) if c == 0 else (y, x + by, c, z))


def other_core(array):
    return send(array, lambda y, x, c, z: (y, x, 1 - c, z))


def along_z(array, by):
    return send(array, lambda y, x, c, z: (y, x, c, z + by))


def between_chips(array):
    count = NY * NX * NC
    pairs = []
    for section in range(1, count - 1):
        partner = section + 1 if section % NC == 1 else section - 1
        pairs += [(section * NZ + z, partner * NZ + z) for z in range(NZ)]
    return lax.ppermute(array, AXES, pairs)


def matmul(left, right):
    return jnp.dot(left, right, preferred_element_type=F32)


def contract(left, right, dims):
    return lax.dot_general(left, right, ((dims[:1], dims[1:]), ((), ())), preferred_element_type=F32)


def softmax_probs(query, *kv_refs):
    scores = jnp.concatenate([contract(query, ref[:, :HEAD_SIZE], (1, 1)) for ref in kv_refs], axis=1)
    scores = scores * (1.0 / math.sqrt(HEAD_SIZE))
    weights = jnp.exp(scores - jnp.max(scores, axis=-1, keepdims=True))
    return weights / jnp.sum(weights, axis=-1, keepdims=True)


def over_rows(left, start_col, *kv_refs):
    total, done = None, 0
    for ref in kv_refs:
        part = matmul(left[:, done : done + ref.shape[0]], ref[:, start_col : start_col + HEAD_SIZE])
        total = part if total is None else total + part
        done += ref.shape[0]
    return total


def on_vmem(kernel, shapes, *operands, place=None, far_in=(), far_out=(), scratch=()):
    vmem, left = pl.BlockSpec(memory_space=pltpu.VMEM), pl.BlockSpec(memory_space=pl.ANY)
    first = [] if place is None else [pl.BlockSpec(memory_space=pltpu.SMEM)]
    outs = [jax.ShapeDtypeStruct(*shape) for shape in shapes]
    held = sum(max(a.size, 8 * 128) * a.dtype.itemsize for a in (*operands, *outs))
    call = pl.pallas_call(
        kernel,
        out_shape=outs,
        in_specs=first + [left if i in far_in else vmem for i in range(len(operands))],
        out_specs=[left if i in far_out else vmem for i in range(len(shapes))],
        scratch_shapes=list(scratch),
        compiler_params=pltpu.CompilerParams(vmem_limit_bytes=held + 3 * 2**20),
        cost_estimate=pl.CostEstimate(flops=2 * 10**9, bytes_accessed=held, transcendentals=0),
    )
    return call(*([] if place is None else [place]), *operands)


def start(source, target, sem):
    copy = pltpu.make_async_copy(source, target, sem)
    copy.start()
    return copy


def stack_kernel(*refs):
    (*parts, out_ref), held, sems = refs[:-2], refs[-2], refs[-1]
    copies, start = [], 0
    for i, ref in enumerate(parts):
        at = pl.ds(start, ref.shape[0])
        into = pltpu.make_async_copy(ref, held.at[at], sems.at[i])
        copies.append((into, pltpu.make_async_copy(held.at[at], out_ref.at[at], sems.at[len(parts) + i])))
        start += ref.shape[0]
    for into, _ in copies:
        into.start()
    for into, out in copies:
        into.wait()
        out.start()
    for _, out in copies:
        out.wait()


def stack(*parts):
    shape = (sum(part.shape[0] for part in parts), parts[0].shape[1])
    hbm = pl.BlockSpec(memory_space=pl.ANY)
    return pl.pallas_call(
        stack_kernel,
        out_shape=jax.ShapeDtypeStruct(shape, parts[0].dtype),
        in_specs=[hbm] * len(parts),
        out_specs=hbm,
        scratch_shapes=[pltpu.VMEM(shape, parts[0].dtype), pltpu.SemaphoreType.DMA((2 * len(parts),))],
        cost_estimate=pl.CostEstimate(flops=1, bytes_accessed=1, transcendentals=0),
    )(*parts)


def heads_kernel(
    all_far, gain_far, wq_far, wo_far, kv_0, kv_1, kv_2, kv_3, d_key_far, d_value_far, out_far,
    all_ref, gain_ref, wq_ref, wo_ref, kv_0_ref, kv_1_ref, kv_2_ref, kv_3_ref, d_key_ref, d_value_ref, out_ref,
    sems,
):
    kv_refs = (kv_0_ref, kv_1_ref, kv_2_ref, kv_3_ref)
    rows, cols = all_ref.shape[0] // 3, out_ref.shape[2]
    width = all_ref.shape[1]
    first_copies, wq_copies = [], []
    for k in range(NZ):
        at = pl.ds(k * cols, cols)
        first_copies.append((
            start(all_far.at[:, at], all_ref.at[:, at], sems.at[0, k]),
            start(wo_far.at[:, at], wo_ref.at[:, at], sems.at[1, k]),
        ))
    gain_copy = start(gain_far, gain_ref, sems.at[3, 0])
    for k in range(NZ):
        at = pl.ds(k * cols, cols)
        wq_copies.append(start(wq_far.at[at], wq_ref.at[at], sems.at[2, k]))
    kv_copies = [start(far, ref, sems.at[3, 1 + i]) for i, (far, ref) in enumerate(zip((kv_0, kv_1, kv_2, kv_3), kv_refs))]

    squares = [jnp.zeros((rows, cols), F32) for _ in range(2)]
    d_att = jnp.zeros((rows, HEAD_SIZE), F32)
    for k in range(NZ):
        at = slice(k * cols, (k + 1) * cols)
        for copy in first_copies[k]:
            copy.wait()
        for block in range(2):
            wide = all_ref[block * rows : (block + 1) * rows, at].astype(F32)
            squares[block] = squares[block] + wide * wide
        d_att = d_att + contract(all_ref[2 * rows :, at], wo_ref[:, at], (1, 1))
    d_att = d_att.astype(BF)
    factors = []
    for block in range(2):
        mean = jnp.sum(squares[block], axis=-1, keepdims=True) * (1.0 / width)
        factors.append(lax.rsqrt(mean + 1e-06))
    out_copies = []
    gain_copy.wait()
    queries = [jnp.zeros((rows, HEAD_SIZE), F32) for _ in range(2)]
    for k in range(NZ):
        at = slice(k * cols, (k + 1) * cols)
        wq_copies[k].wait()
        for block in range(2):
            normed = all_ref[block * rows : (block + 1) * rows, at].astype(F32) * factors[block] * gain_ref[:, at]
            queries[block] = queries[block] + matmul(normed.astype(BF), wq_ref[at, :])

    for copy in kv_copies:
        copy.wait()
    query = queries[1].astype(BF)
    probs = softmax_probs(query, *kv_refs)
    d_probs = jnp.concatenate([contract(d_att, ref[:, HEAD_SIZE:], (1, 1)) for ref in kv_refs], axis=1)
    inner = jnp.sum(probs * d_probs, axis=-1, keepdims=True)
    d_score = (probs * (d_probs - inner) * (1.0 / math.sqrt(HEAD_SIZE))).astype(BF)
    d_key_ref[...] = contract(d_score, query, (0, 0)).astype(BF)
    out_copies.append(start(d_key_ref, d_key_far, sems.at[3, 6]))
    d_value_ref[...] = contract(probs.astype(BF), d_att, (0, 0)).astype(BF)
    out_copies.append(start(d_value_ref, d_value_far, sems.at[3, 7]))
    d_query = over_rows(d_score, 0, *kv_refs).astype(BF)
    extra_rows = out_ref.shape[1] - 2 * rows
    sums = lax.dot_general(
        jnp.ones((extra_rows, HEAD_SIZE), F32),
        d_query.astype(F32) * queries[1] * (factors[1] * factors[1] * (1.0 / width)),
        (((1,), (1,)), ((), ())),
        precision=lax.Precision.HIGHEST,
        preferred_element_type=F32,
    )
    sums = jnp.concatenate([sums, jnp.zeros((extra_rows, cols - rows), F32)], axis=1).astype(BF)

    probs = softmax_probs(queries[0].astype(BF), *kv_refs).astype(BF)
    attended = over_rows(probs, HEAD_SIZE, *kv_refs).astype(BF)
    for k in range(NZ):
        at = slice(k * cols, (k + 1) * cols)
        out_ref[k, :rows] = (contract(d_query, wq_ref[at, :], (1, 1)) * factors[1]).astype(BF)
        out_ref[k, rows : 2 * rows] = matmul(attended, wo_ref[:, at]).astype(BF)
        out_ref[k, 2 * rows :] = sums
        out_copies.append(start(out_ref.at[k], out_far.at[k], sems.at[4, k]))
    for copy in out_copies:
        copy.wait()


def memory_part(d_key, d_value, wk_ref, wv_ref, out_refs, *added):
    width, tile = wk_ref.shape[0], 512

    def tile_of(refs, k):
        ref = refs[k * tile * len(refs) // width]
        at = k * tile % ref.shape[1]
        return ref, slice(at, at + tile)

    for k in range(width // tile):
        at = slice(k * tile, (k + 1) * tile)
        part = contract(d_key, wk_ref[at, :], (1, 1)) + contract(d_value, wv_ref[at, :], (1, 1))
        for refs in added:
            ref, cols = tile_of(refs, k)
            part = part + ref[:, cols].astype(F32)
        ref, cols = tile_of(out_refs, k)
        ref[:, cols] = part.astype(ref.dtype)


def finish_kernel(place_ref, sums_ref, x_ref, h_ref, g_ref, gain_ref, same_ref, next_ref):
    rows, cols = x_ref.shape
    layer_out = (x_ref[...].astype(F32) + sums_ref[rows : 2 * rows].astype(F32)).astype(BF)
    at = pl.multiple_of(lax.rem(place_ref[0], NZ) * cols, cols)
    gain = gain_ref[:, pl.ds(at, cols)]
    eye = lax.broadcasted_iota(jnp.int32, (rows, rows), 0) == lax.broadcasted_iota(jnp.int32, (rows, rows), 1)
    inner = contract(jnp.where(eye, 1.0, 0.0).astype(BF), sums_ref[2 * rows :, :rows], (1, 1))[:, :1]
    d_in = g_ref[...].astype(F32) + gain * sums_ref[:rows].astype(F32)
    d_in = (d_in - h_ref[...].astype(F32) * inner).astype(BF)

    @pl.when(place_ref[0] < NZ)
    def _():
        same_ref[...] = layer_out
        next_ref[...] = d_in

    @pl.when(place_ref[0] >= NZ)
    def _():
        same_ref[...] = d_in
        next_ref[...] = layer_out


def cross_kernel(blocks, d_key_ref, d_value_ref, wk_ref, wv_ref, *refs):
    for i, ref in zip(blocks, refs[-len(blocks) :]):
        at = slice((4 + i) * ref.shape[0], (5 + i) * ref.shape[0])
        memory_part(d_key_ref[at], d_value_ref[at], wk_ref, wv_ref, [ref])


def halves_kernel(columns_from, d_key_ref, d_value_ref, wk_ref, wv_ref, *refs):
    rows = refs[-1].shape[0]
    at = slice(columns_from * rows, (columns_from + 1) * rows)
    memory_part(d_key_ref[at], d_value_ref[at], wk_ref, wv_ref, refs[-2:], refs[:-2])


def middle_kernel(d_key_ref, d_value_ref, wk_ref, wv_ref, low_ref, high_ref, out_low, out_high):
    rows, cols = out_low.shape
    width, tile = wk_ref.shape[0], 512
    for block, ref, arrived, start in ((1, out_low, low_ref, cols), (2, out_high, high_ref, 0)):
        rows_at = slice(block * rows, (block + 1) * rows)
        for k in range(cols // tile):
            at = slice(start + k * tile, start + (k + 1) * tile)
            part = contract(d_key_ref[rows_at], wk_ref[at, :], (1, 1))
            part = part + contract(d_value_ref[rows_at], wv_ref[at, :], (1, 1))
            ref[:, k * tile : (k + 1) * tile] = (part + arrived[:, at].astype(F32)).astype(ref.dtype)


def edge_kernel(d_key_ref, d_value_ref, wk_ref, wv_ref, low_ref, high_ref, add_low, add_high, out_low, out_high):
    rows, cols = out_low.shape
    width, tile = wk_ref.shape[0], 512
    for block, ref, arrived, add, start in ((1, out_low, low_ref, add_low, 0), (2, out_high, high_ref, add_high, cols)):
        rows_at = slice(block * rows, (block + 1) * rows)
        for k in range(cols // tile):
            at = slice(start + k * tile, start + (k + 1) * tile)
            here = slice(k * tile, (k + 1) * tile)
            part = contract(d_key_ref[rows_at], wk_ref[at, :], (1, 1))
            part = part + contract(d_value_ref[rows_at], wv_ref[at, :], (1, 1))
            part = part + arrived[:, at].astype(F32) + add[:, here].astype(F32)
            ref[:, here] = part.astype(ref.dtype)


def near_kernel(d_key_ref, d_value_ref, wk_ref, wv_ref, arrived_ref, out_ref):
    rows = arrived_ref.shape[0]
    memory_part(d_key_ref[:rows], d_value_ref[:rows], wk_ref, wv_ref, [out_ref], [arrived_ref])


def collect_kernel(near_ref, low_a, low_b, high_a, high_b, mine_ref, *wires):
    mine, cols, tile = mine_ref.shape[0], low_a.shape[1], 512
    for k in range(near_ref.shape[1] // tile):
        at = slice(k * tile, (k + 1) * tile)
        low, high = (low_a, high_a) if k * tile < cols else (low_b, high_b)
        here = slice(k * tile % cols, k * tile % cols + tile)
        total = near_ref[:, at] + low[:, here].astype(F32) + high[:, here].astype(F32)
        for i, ref in enumerate((mine_ref, *wires)):
            ref[:, at] = total[i * mine : (i + 1) * mine].astype(ref.dtype)


def assemble_kernel(a_ref, b_ref, c_ref, d_ref, first_ref, second_ref, near_ref):
    mine, cols = a_ref.shape[0], first_ref.shape[1]
    for i, ref in enumerate((a_ref, b_ref, c_ref, d_ref)):
        at = slice(i * mine, (i + 1) * mine)
        first_ref[at] = ref[:, :cols]
        second_ref[at] = ref[:, cols:]
        near_ref[at] = ref[...]


def keys_kernel(count, *refs):
    pieces, wk_ref, wv_ref, out_ref = refs[:count], refs[count], refs[count + 1], refs[-1]
    rows, width, tile = pieces[0].shape[0], wk_ref.shape[0], 1024
    blocks = []
    while pieces:
        count = width // pieces[0].shape[1]
        blocks.append(pieces[:count])
        pieces = pieces[count:]
    for i, block in enumerate(blocks):
        for w_ref, at in ((wk_ref, 0), (wv_ref, HEAD_SIZE)):
            total = jnp.zeros((rows, HEAD_SIZE), F32)
            for k in range(width // tile):
                ref = block[k * tile * len(block) // width]
                here = k * tile % ref.shape[1]
                total = total + matmul(ref[:, here : here + tile], w_ref[k * tile : (k + 1) * tile, :])
            out_ref[i * rows : (i + 1) * rows, at : at + HEAD_SIZE] = total.astype(BF)


def spread_kernel(mine_ref, a_ref, b_ref, c_ref, block_ref, grad_ref, out_ref):
    rows, cols = mine_ref.shape[0], out_ref.shape[1]
    for k in range(NZ):
        at = slice(k * cols, (k + 1) * cols)
        total = mine_ref[:, at] + a_ref[:, at].astype(F32) + b_ref[:, at].astype(F32) + c_ref[:, at].astype(F32)
        out_ref[k * rows : (k + 1) * rows] = total.astype(BF)


def total_kernel(place_ref, parts_ref, same_ref, next_ref, out_ref, block_out, grad_out):
    rows = out_ref.shape[0]
    total = parts_ref[:rows].astype(F32)
    for k in range(1, NZ):
        total = total + parts_ref[k * rows : (k + 1) * rows].astype(F32)
    out_ref[...] = total

    @pl.when(place_ref[0] < NZ)
    def _():
        block_out[...] = next_ref[...]
        grad_out[...] = same_ref[...]

    @pl.when(place_ref[0] >= NZ)
    def _():
        block_out[...] = same_ref[...]
        grad_out[...] = next_ref[...]


def body(block_in, saved_in, block_grad, memory, norm_gain, w_query, w_key, w_value, w_out):
    rows, cols = block_in.shape
    width, size = w_query.shape[1:]
    at_z = (lax.axis_index("tensor") + NZ * lax.rem(lax.axis_index("section"), NC)).reshape(1)

    gathered = lax.all_gather(stack(block_in, saved_in, block_grad), "tensor", axis=1, tiled=True)
    wq, wk, wv, wo = w_query[0], w_key[0], w_value[0], w_out[0]

    mem = NY * NX * NC * memory.shape[0]
    quarter = mem // 8
    half = ((quarter, width // 2), BF)
    near_a, near_b, near = on_vmem(
        assemble_kernel, [half] * 2 + [((quarter, width), BF)], memory, first_axis(memory, 1), first_axis(memory, -1), first_axis(memory, 2)
    )
    low_a, high_b = second_axis(near_a, 1), second_axis(near_b, -1)
    low_b, high_a = second_axis(near_b, 1), second_axis(near_a, -1)
    far_a, far_b = second_axis(low_a, 1), second_axis(high_b, -1)

    near_sent, low_a, high_b = lax.optimization_barrier((near, low_a, high_b))
    others = [other_core(piece) for piece in (near_sent, low_a, low_b, high_a, high_b)]

    def keys_of(*pieces):
        blocks = sum(piece.shape[1] for piece in pieces) // width
        kernel = functools.partial(keys_kernel, len(pieces))
        return on_vmem(kernel, [((blocks * quarter, 2 * size), BF)], *pieces, wk, wv)[0]

    kv = (
        keys_of(near, low_a, low_b, high_a, high_b),
        keys_of(far_a, far_b),
        keys_of(*others),
        keys_of(other_core(far_a), other_core(far_b)),
    )

    ins = (gathered, norm_gain, wq, wo, *kv)
    outs = [((mem, size), BF), ((mem, size), BF), ((NZ, 2 * rows + 16, cols), BF)]
    far = pl.BlockSpec(memory_space=pltpu.HBM)
    d_key, d_value, sent = pl.pallas_call(
        heads_kernel,
        out_shape=[jax.ShapeDtypeStruct(*out) for out in outs],
        in_specs=[far] * len(ins),
        out_specs=[far] * len(outs),
        scratch_shapes=[pltpu.VMEM(a.shape, a.dtype) for a in ins]
        + [pltpu.VMEM(*out) for out in outs]
        + [pltpu.SemaphoreType.DMA((5, NZ))],
        compiler_params=pltpu.CompilerParams(vmem_limit_bytes=60 * 2**20),
        cost_estimate=pl.CostEstimate(flops=4 * 10**9, bytes_accessed=12 * 2**20, transcendentals=0),
    )(*ins)
    summed = lax.psum_scatter(sent, "tensor", scatter_dimension=0, tiled=True)[0]
    to_same, to_next = on_vmem(
        finish_kernel, [((rows, cols), BF)] * 2, summed, block_in, saved_in, block_grad, norm_gain,
        place=at_z,
    )
    same, crossed = other_core(to_same), between_chips(to_next)

    mine = memory.shape[0]
    own = (d_key, d_value, wk, wv)
    whole = ((quarter, width), BF)

    def cross(blocks, *after):
        kernel = functools.partial(cross_kernel, blocks)
        return [other_core(block) for block in on_vmem(kernel, [whole] * len(blocks), *own, *after)]

    (far,) = cross((3,))
    low, high = cross((1, 2))
    far_a, far_b = on_vmem(functools.partial(halves_kernel, 3), [half] * 2, *own, far)
    (near,) = cross((0,), far_a)
    low_b, high_a = on_vmem(middle_kernel, [half] * 2, *own, low, high)
    back_low_b, back_high_a = second_axis(low_b, -1), second_axis(high_a, 1)
    low_a, high_b = on_vmem(
        edge_kernel, [half] * 2, *own, low, high, second_axis(far_a, -1), second_axis(far_b, 1)
    )
    back_low_a, back_high_b = second_axis(low_a, -1), second_axis(high_b, 1)
    (near,) = on_vmem(near_kernel, [((quarter, width), F32)], *own, near)
    t_mine, *wires = on_vmem(
        collect_kernel,
        [((mine, width), F32)] + [((mine, width), BF)] * 3,
        near, back_low_a, back_low_b, back_high_a, back_high_b,
    )
    arrived = [first_axis(wires[0], -1), first_axis(wires[1], 1), first_axis(wires[2], 2)]
    (spread,) = on_vmem(spread_kernel, [((NZ * mine, cols), BF)], t_mine, *arrived, to_same, to_next)
    parts = lax.all_to_all(spread, "tensor", 0, 0, tiled=True)
    memory_grad, next_block, prev_grad = on_vmem(
        total_kernel, [((mine, cols), F32)] + [((rows, cols), BF)] * 2, parts, same, crossed, place=at_z
    )
    return next_block, prev_grad, memory_grad


def solution(mesh):
    in_specs = (
        P("section", "tensor"),
        P("section", "tensor"),
        P("section", "tensor"),
        P("section", None),
        P("section", None),
        P("section", None, "tensor"),
        P("section", None, "tensor"),
        P("section", None, "tensor"),
        P("section", "tensor", None),
    )
    out_specs = (P("section", "tensor"), P("section", "tensor"), P("section", "tensor"))
    return jax.shard_map(body, mesh=mesh, in_specs=in_specs, out_specs=out_specs, check_vma=False)
```
